256 devices in a mesh: worker: 4 (over z_hi), fsdp: 64 (over y, x, z_lo, core).
Axes of the slice: x: 4, y: 4, z: 8 (z_hi: 4, z_lo: 2; z = z_hi * 2 + z_lo), core: 2. Of those that a mesh axis runs over, the one named last changes fastest.
Arguments:
- inner_input: bfloat16 [4, 32768, 4608], P('worker', 'fsdp'), may hold values from -16 to 16
- inner_weight: bfloat16 [4, 4608, 1024], P('worker', 'fsdp'), may hold values from -6 to 6
- grad_out: bfloat16 [4, 32768, 1024], P('worker', 'fsdp'), may hold values from -6 to 6
- local_fragment: bfloat16 [4, 4608, 18432], P('worker', 'fsdp'), may hold values from -6 to 6
- anchor: bfloat16 [4608, 18432], P('fsdp'), may hold values from -6 to 6
- momentum: float32 [4608, 18432], P('fsdp', 'worker'), may hold values from -6 to 6
Outputs:
- weight_grad: float32 [4, 4608, 1024], P('worker', 'fsdp')
- new_anchor: bfloat16 [4608, 18432], P('fsdp', 'worker')
- new_momentum: float32 [4608, 18432], P('fsdp', 'worker')
The draws below stay inside these ranges and needn't reach their ends.
All inputs are finite; a program needn't handle non-finite values.
Results may differ from the reference program's by a relative error of at most 0.0035.
Values may be sent and summed in bfloat16 or wider, within the bound.
A program may use at most 128 MiB of HBM per device.

```python
import jax
import jax.numpy as jnp
from jax import lax

D = 4608
FW = 18432
KW = 1024
QBLOCK = 32
WORKERS = 4
TOKENS = 32768


def spiked(values, own_key, source, target, shards_of, factor):
    owner, partner = [(jnp.arange(values.shape[axis_at]) // (values.shape[axis_at] // shards_of)).reshape([-1 if axis == axis_at else 1 for axis in range(values.ndim)]) for axis_at in (source, target)]
    chosen = jax.random.permutation(own_key, shards_of)[partner]
    strong = (owner == chosen) | (owner == (partner + shards_of // 2) % shards_of)
    return jnp.where(strong, factor * values, values)


def level_of(rng, shape, shards, low, largest):
    def one(axis_at, blocks):
        steps = jax.random.uniform(jax.random.fold_in(jax.random.fold_in(rng, 6), axis_at), (blocks,), jnp.float32, low / len(shards), largest / len(shards))
        return jnp.repeat(jnp.exp(steps), shape[axis_at] // blocks).reshape((-1,) + (1,) * (len(shape) - axis_at - 1))

    factor_of = one(*shards[0])
    for cut in shards[1:]:
        factor_of = factor_of * one(*cut)
    return factor_of


def gaussian(own_key, extent, scale, reach, split=(), kind=jnp.bfloat16):
    entries = jax.random.normal(own_key, extent, jnp.float32) * scale
    if len(split) > 0:
        entries = level_of(own_key, extent, split, -0.22, 0.18) * entries
    return jnp.clip(entries, min=-reach, max=reach).astype(kind)


def gaussian_with(key, dims, scale, most, cuts, heavy, kind=jnp.bfloat16):
    drawn = scale * jax.random.normal(key, dims, jnp.float32)
    if cuts:
        drawn = drawn * level_of(key, dims, cuts, -0.22, 0.18)
    return jnp.clip(spiked(drawn, jax.random.fold_in(key, 3), *heavy), -most, most).astype(kind)


def setup_inputs(seed: int = 0) -> dict:
    key_list = jax.random.split(jax.random.key(seed), 7)
    return {
        "inner_input": gaussian_with(key_list[0], (WORKERS, TOKENS, D), 1.0, 16.0, ((0, 4), (1, 64)), (1, 2, 64, 4.0)),
        "inner_weight": gaussian(key_list[1], (WORKERS, D, KW), 1.0, 6.0, ((0, 4), (1, 64))),
        "grad_out": gaussian(key_list[2], (WORKERS, TOKENS, KW), 1.0, 6.0, ((0, 4), (1, 64))),
        "local_fragment": gaussian(key_list[3], (WORKERS, D, FW), 1.0, 6.0, ((0, 4), (1, 64))),
        "anchor": gaussian(key_list[4], (D, FW), 1.0, 6.0, ((0, 64),)),
        "momentum": gaussian(key_list[5], (D, FW), 1.0, 6.0, ((0, 64), (1, 4)), jnp.float32),
    }


def e2m1_level(u):
    level = 0.5 * (u >= 0.25) + 0.5 * (u >= 0.75) + 0.5 * (u >= 1.25) + 0.5 * (u >= 1.75)
    level = level + 1.0 * (u >= 2.5) + 1.0 * (u >= 3.5) + 2.0 * (u >= 5.0)
    return level.astype(u.dtype)

def code_delta(local, anchor):
    delta = anchor.astype(jnp.float32) - local.astype(jnp.float32)
    rows_n, cols_n = delta.shape
    blocks = delta.reshape(rows_n, cols_n // QBLOCK, QBLOCK)
    top = lax.optimization_barrier(jnp.max(jnp.abs(blocks), axis=2, keepdims=True))
    step = jnp.exp2(jnp.ceil(jnp.log2(top))) * 0.25
    level = e2m1_level(jnp.abs(blocks) / step)
    return (jnp.sign(blocks) * level * step).reshape(rows_n, cols_n)

def inner_grad(inputs):
    x, weight, dy = inputs
    factor = D ** (-0.5)
    pre = jnp.dot(x, weight, preferred_element_type=jnp.float32) * factor
    sig = jax.nn.sigmoid(pre)
    act_grad = (dy.astype(jnp.float32) * sig * (1.0 + pre * (1.0 - sig))).astype(jnp.bfloat16)
    return jnp.dot(x.T, act_grad, preferred_element_type=jnp.float32) * factor

def reference(inner_input, inner_weight, grad_out, local_fragment, anchor, momentum):
    weight_grad = lax.map(inner_grad, (inner_input, inner_weight, grad_out))

    def accumulate(total, local):
        return (total + code_delta(local, anchor), None)
    total, unused = lax.scan(accumulate, jnp.zeros(anchor.shape, jnp.float32), local_fragment)
    outer_grad = total / WORKERS
    new_momentum = 0.9 * momentum + outer_grad
    new_anchor = (anchor.astype(jnp.float32) - 0.7 * (outer_grad + 0.9 * new_momentum)).astype(jnp.bfloat16)
    return (weight_grad, new_anchor, new_momentum)
```

```python
import jax
import jax.numpy as jnp
from jax import lax
from jax.experimental import pallas as pl
from jax.experimental.pallas import tpu as pltpu
from jax.sharding import PartitionSpec as P

F32 = jnp.float32
BF16 = jnp.bfloat16
MESH = pl.DeviceIdType.MESH

TOK = 512
D = 4608
HALF = 512
Q = 256
YB = 1152
XB = 288
ROWS = 72
WC = 4608
WH = 2304


def ring(i):
    return lax.rem(i + 1, 4), lax.rem(i + 3, 4), lax.rem(i + 2, 4)


def coded_of(local, anchor):
    delta = anchor.astype(F32) - local.astype(F32)
    mag = jnp.abs(delta)
    lane = lax.broadcasted_iota(jnp.int32, mag.shape, 1)
    top = mag
    for s in (1, 2, 4, 8, 16):
        top = jnp.maximum(top, pltpu.roll(top, s, 1))
    top = jnp.where(lax.rem(lane, 32) == 31, top, 0.0)
    for s in (1, 2, 4, 8, 16):
        top = jnp.maximum(top, pltpu.roll(top, 128 - s, 1))
    q = top * (2.0**23 + 1.0)
    low = jnp.abs(q - q * (1.0 - 2.0**-24))
    step = jnp.where(low < top, low * 0.5, low * 0.25)
    level = jnp.where(mag >= 0.25 * step, 0.5, 0.0)
    level = jnp.where(mag >= 0.75 * step, 1.0, level)
    level = jnp.where(mag >= 1.25 * step, 1.5, level)
    level = jnp.where(mag >= 1.75 * step, 2.0, level)
    level = jnp.where(mag >= 2.5 * step, 3.0, level)
    level = jnp.where(mag >= 3.5 * step, 4.0, level)
    level = jnp.where(mag >= 5.0 * step, 6.0, level)
    coded = level * step
    return jnp.where(delta < 0, -coded, coded).astype(BF16)


def kernel(
    x_in, w_in, g_in, loc_in, anc_in, mom_in,
    wg_out, na_out, nm_out,
    xs, gs, wraw, wa, wb, pre, act, pa, pb,
    ra_o, ra_l, ra_r, rb_o, rb_l, rb_r,
    sa, sb, sa16, sb16,
    ta_o, ta_l, ta_r, tb_o, tb_l, tb_r,
    tt, fs_send, fs_recv, fz_send, fz_recv, wg_v,
    loc, anc, mom, cod, wo, wl, wr, na_v, nm_v,
    lsem, ssem, rsem,
):
    me = lax.axis_index("fsdp")
    wk = lax.axis_index("worker")
    c = lax.rem(me, 2)
    z = lax.rem(me // 2, 2)
    x = lax.rem(me // 4, 4)
    y = me // 16
    xr, xl, xo = ring(x)
    yr, yl, yo = ring(y)
    wr_i, wl_i, wo_i = ring(wk)

    def dev(yy, xx, zz, cc):
        return (wk, ((yy * 4 + xx) * 2 + zz) * 2 + cc)

    sib = dev(y, x, z, 1 - c)
    zsame = dev(y, x, 1 - z, c)
    zother = dev(y, x, 1 - z, 1 - c)
    xright, xleft = dev(y, xr, z, c), dev(y, xl, z, c)
    yright, yleft = dev(yr, x, z, c), dev(yl, x, z, c)
    wright, wleft = (wr_i, me), (wl_i, me)

    pending = []
    count = [0]

    def send(src, dst, to):
        k = count[0]
        count[0] += 1
        copy = pltpu.make_async_remote_copy(
            src_ref=src, dst_ref=dst, send_sem=ssem.at[k], recv_sem=rsem.at[k],
            device_id=to, device_id_type=MESH,
        )
        copy.start()
        pending.append(copy)
        return copy

    lcount = [0]

    def local(src, dst):
        k = lcount[0]
        lcount[0] += 1
        copy = pltpu.make_async_copy(src, dst, lsem.at[k])
        copy.start()
        return copy

    def cols(j):
        return pl.ds(pl.multiple_of(j * HALF, HALF), HALF)

    def wcols(j):
        return pl.ds(pl.multiple_of(j * WC, 128), WC)

    def xrows(j):
        return pl.ds(pl.multiple_of(j * XB, 16), XB)

    def xrows_half(j, h):
        return pl.ds(pl.multiple_of(j * XB + h * (XB // 2), 16), XB // 2)

    own_w = local(w_in.at[:, cols(c)], wraw.at[z, c])
    frag = {}
    for name, j in (("o", wo_i), ("r", wr_i), ("l", wl_i), ("s", wk)):
        frag[name] = (
            local(loc_in.at[:, wcols(j)], loc.at[j]),
            local(anc_in.at[:, wcols(j)], anc.at[j]),
        )
    own_x = local(x_in, xs.at[0])
    own_g = local(g_in.at[:, cols(c)], gs.at[0])
    own_m = local(mom_in, mom)

    barrier = pltpu.get_barrier_semaphore()
    partners = (sib, zsame, zother, xright, xleft, yright, yleft, wright, wleft)
    for p in partners:
        pl.semaphore_signal(barrier, inc=1, device_id=p, device_id_type=MESH)
    pl.semaphore_wait(barrier, len(partners))

    g1 = send(w_in.at[:, cols(c)], wraw.at[z, c], zsame)
    g2 = send(w_in.at[:, cols(1 - c)], wraw.at[z, c], zother)
    g0 = send(w_in.at[:, cols(1 - c)], wraw.at[z, c], sib)
    sx = send(x_in, xs.at[1], sib)
    sg = send(g_in.at[:, cols(1 - c)], gs.at[1], sib)

    def code_block(name, j):
        for copy in frag[name]:
            copy.wait()
        for h in range(2):
            def body(i, carry, h=h):
                at = pl.multiple_of(h * WH + i * 128, 128)
                to = pl.multiple_of(i * 128, 128)
                cod[j, h, :, pl.ds(to, 128)] = coded_of(
                    loc[j, :, pl.ds(at, 128)], anc[j, :, pl.ds(at, 128)]
                )
                return carry
            lax.fori_loop(0, WH // 128, body, 0)

    code_block("o", wo_i)
    w0 = send(cod.at[wo_i, 0], wo.at[0], wright)
    w1 = send(cod.at[wo_i, 1], wo.at[1], wleft)

    own_w.wait()
    for copy in (g1, g2, g0):
        copy.wait_recv()
    for zz in range(2):
        rows = jnp.concatenate(
            [wraw[zz, 0].astype(F32), wraw[zz, 1].astype(F32)], axis=0
        ).astype(BF16)
        wa[y, xrows_half(x, zz), :] = rows[:, :Q]
        wb[y, xrows_half(x, zz), :] = rows[:, Q:]

    a1 = send(wa.at[y, xrows(x)], wa.at[y, xrows(x)], xright)
    a2 = send(wa.at[y, xrows(x)], wa.at[y, xrows(x)], xleft)
    b1 = send(wb.at[y, xrows(x)], wb.at[y, xrows(x)], yright)
    b2 = send(wb.at[y, xrows(x)], wb.at[y, xrows(x)], yleft)

    code_block("r", wr_i)
    w2 = send(cod.at[wr_i, 1], wl.at[1], wright)

    a1.wait_recv()
    a3 = send(wa.at[y, xrows_half(xl, 0)], wa.at[y, xrows_half(xl, 0)], xright)
    b1.wait_recv()
    b3 = send(wb.at[yl, xrows_half(x, 0)], wb.at[yl, xrows_half(x, 0)], yright)
    a2.wait_recv()
    a4 = send(wa.at[y, xrows_half(xr, 1)], wa.at[y, xrows_half(xr, 1)], xleft)
    b2.wait_recv()
    b4 = send(wb.at[yr, xrows_half(x, 1)], wb.at[yr, xrows_half(x, 1)], yleft)

    code_block("l", wl_i)
    w3 = send(cod.at[wl_i, 0], wr.at[0], wleft)

    a3.wait_recv()
    a4.wait_recv()
    a5 = send(wa.at[y], wa.at[y], yright)
    a6 = send(wa.at[y], wa.at[y], yleft)
    b3.wait_recv()
    b4.wait_recv()
    b5 = send(wb.at[:, xrows(x)], wb.at[:, xrows(x)], xright)
    b6 = send(wb.at[:, xrows(x)], wb.at[:, xrows(x)], xleft)

    code_block("s", wk)

    def project(w, yy, col, first):
        def body(i, carry):
            t = i // 2
            r = pl.ds(pl.multiple_of(lax.rem(i, 2) * 256, 256), 256)
            lhs = xs[t, r, pl.ds(pl.multiple_of(yy * YB, 128), YB)]
            part = jnp.dot(lhs, w[yy], preferred_element_type=F32)
            if first:
                pre[t, r, col:col + Q] = part
            else:
                pre[t, r, col:col + Q] += part
            return carry
        lax.fori_loop(0, 4, body, 0)

    own_x.wait()
    sx.wait_recv()
    project(wa, y, 0, True)

    a5.wait_recv()
    a7 = send(wa.at[yl, 0:YB // 2], wa.at[yl, 0:YB // 2], yright)
    a6.wait_recv()
    a8 = send(wa.at[yr, YB // 2:YB], wa.at[yr, YB // 2:YB], yleft)
    b5.wait_recv()
    b7 = send(wb.at[0:2, xrows(xl)], wb.at[0:2, xrows(xl)], xright)
    b6.wait_recv()
    b8 = send(wb.at[2:4, xrows(xr)], wb.at[2:4, xrows(xr)], xleft)

    w0.wait_recv()
    w1.wait_recv()
    for j, h in ((wr_i, 0), (wl_i, 1)):
        def body(i, carry, j=j, h=h):
            at = pl.ds(pl.multiple_of(i * 256, 256), 256)
            cod[j, h, :, at] = (cod[j, h, :, at].astype(F32) + wo[h, :, at].astype(F32)).astype(BF16)
            return carry
        lax.fori_loop(0, WH // 256, body, 0)
    w4 = send(cod.at[wr_i, 0], wl.at[0], wright)
    w5 = send(cod.at[wl_i, 1], wr.at[1], wleft)

    project(wa, yl, 0, False)
    project(wa, yr, 0, False)
    a7.wait_recv()
    a8.wait_recv()
    project(wa, yo, 0, False)
    b7.wait_recv()
    b8.wait_recv()
    project(wb, 0, Q, True)
    for yy in (1, 2, 3):
        project(wb, yy, Q, False)

    own_g.wait()
    sg.wait_recv()
    factor = D ** (-0.5)

    def activate(i, carry):
        t = i // 8
        r = pl.ds(pl.multiple_of(lax.rem(i, 8) * 64, 64), 64)
        value = pre[t, r, :] * factor
        sig = jax.nn.sigmoid(value)
        act[t, r, :] = (gs[t, r, :].astype(F32) * sig * (1.0 + value * (1.0 - sig))).astype(BF16)
        return carry

    lax.fori_loop(0, 16, activate, 0)

    def backward(yy, out, col):
        def body(i, carry):
            at = pl.ds(pl.multiple_of(yy * YB + i * 384, 128), 384)
            dims = (((0,), (0,)), ((), ()))
            part = lax.dot_general(xs[0, :, at], act[0, :, col:col + Q], dims, preferred_element_type=F32)
            part += lax.dot_general(xs[1, :, at], act[1, :, col:col + Q], dims, preferred_element_type=F32)
            out[yy, pl.ds(pl.multiple_of(i * 384, 384), 384), :] = part.astype(BF16)
            return carry
        lax.fori_loop(0, 3, body, 0)

    hy = YB // 2
    backward(yo, pa, 0)
    ra0 = send(pa.at[yo, 0:hy], ra_o.at[0], yright)
    ra1 = send(pa.at[yo, hy:YB], ra_o.at[1], yleft)
    backward(yr, pa, 0)
    ra2 = send(pa.at[yr, hy:YB], ra_l.at[hy:YB], yright)
    backward(yl, pa, 0)
    ra3 = send(pa.at[yl, 0:hy], ra_r.at[0:hy], yleft)
    for yy in range(4):
        backward(yy, pb, Q)
    rb0 = send(pb.at[0:2, xrows(xo)], rb_o.at[0], xright)
    rb1 = send(pb.at[2:4, xrows(xo)], rb_o.at[1], xleft)
    rb2 = send(pb.at[2:4, xrows(xr)], rb_l.at[2:4], xright)
    rb3 = send(pb.at[0:2, xrows(xl)], rb_r.at[0:2], xleft)
    backward(y, pa, 0)

    def add_rows(dst, at, other, n):
        def body(i, carry):
            r = pl.ds(pl.multiple_of(i * 96, 16), 96)
            d = pl.ds(pl.multiple_of(at[1] + i * 96, 16), 96)
            dst[at[0], d, :] = (dst[at[0], d, :].astype(F32) + other(r).astype(F32)).astype(BF16)
            return carry
        lax.fori_loop(0, n // 96, body, 0)

    ra0.wait_recv()
    add_rows(pa, (yr, 0), lambda r: ra_o[0, r, :], hy)
    ra4 = send(pa.at[yr, 0:hy], ra_l.at[0:hy], yright)
    ra1.wait_recv()
    add_rows(pa, (yl, hy), lambda r: ra_o[1, r, :], hy)
    ra5 = send(pa.at[yl, hy:YB], ra_r.at[hy:YB], yleft)
    rb0.wait_recv()
    for k in range(2):
        add_rows(pb, (k, xr * XB), lambda r, k=k: rb_o[0, k, r, :], XB)
    rb4 = send(pb.at[0:2, xrows(xr)], rb_l.at[0:2], xright)
    rb1.wait_recv()
    for k in range(2):
        add_rows(pb, (2 + k, xl * XB), lambda r, k=k: rb_o[1, k, r, :], XB)
    rb5 = send(pb.at[2:4, xrows(xl)], rb_r.at[2:4], xleft)

    for copy in (w2, w3, w4, w5):
        copy.wait_recv()
    own_m.wait()
    for h in range(2):
        def outer(i, carry, h=h):
            at = pl.ds(pl.multiple_of(i * 128, 128), 128)
            to = pl.ds(pl.multiple_of(h * WH + i * 128, 128), 128)
            total = cod[wk, h, :, at].astype(F32) + wl[h, :, at].astype(F32) + wr[h, :, at].astype(F32)
            grad = total * 0.25
            fresh = 0.9 * mom[:, to] + grad
            nm_v[:, to] = fresh
            na_v[:, to] = (anc[wk, :, to].astype(F32) - 0.7 * (grad + 0.9 * fresh)).astype(BF16)
            return carry
        lax.fori_loop(0, WH // 128, outer, 0)
    out1 = local(na_v, na_out)
    out2 = local(nm_v, nm_out)

    for copy in (ra2, ra3, ra4, ra5):
        copy.wait_recv()

    def sum_a(i, carry):
        r = pl.ds(pl.multiple_of(i * 96, 96), 96)
        total = pa[y, r, :].astype(F32) + ra_l[r, :].astype(F32) + ra_r[r, :].astype(F32)
        sa[r, :] = total
        sa16[r, :] = total.astype(BF16)
        return carry

    lax.fori_loop(0, YB // 96, sum_a, 0)
    hx = XB // 2
    ta0 = send(sa16.at[xrows_half(xo, 0)], ta_o.at[0], xright)
    ta1 = send(sa16.at[xrows_half(xo, 1)], ta_o.at[1], xleft)
    ta2 = send(sa16.at[xrows_half(xr, 1)], ta_l.at[hx:XB], xright)
    ta3 = send(sa16.at[xrows_half(xl, 0)], ta_r.at[0:hx], xleft)

    for copy in (rb2, rb3, rb4, rb5):
        copy.wait_recv()

    def sum_b(i, carry):
        k = i // 3
        r = pl.ds(pl.multiple_of(lax.rem(i, 3) * 96, 96), 96)
        at = pl.ds(pl.multiple_of(x * XB + lax.rem(i, 3) * 96, 16), 96)
        total = pb[k, at, :].astype(F32) + rb_l[k, r, :].astype(F32) + rb_r[k, r, :].astype(F32)
        sb[k, r, :] = total
        sb16[k, r, :] = total.astype(BF16)
        return carry

    lax.fori_loop(0, 12, sum_b, 0)
    tb0 = send(sb16.at[yo, 0:hx], tb_o.at[0], yright)
    tb1 = send(sb16.at[yo, hx:XB], tb_o.at[1], yleft)
    tb2 = send(sb16.at[yr, hx:XB], tb_l.at[hx:XB], yright)
    tb3 = send(sb16.at[yl, 0:hx], tb_r.at[0:hx], yleft)

    ta0.wait_recv()
    sa16[xrows_half(xr, 0), :] = (sa[xrows_half(xr, 0), :] + ta_o[0].astype(F32)).astype(BF16)
    ta4 = send(sa16.at[xrows_half(xr, 0)], ta_l.at[0:hx], xright)
    ta1.wait_recv()
    sa16[xrows_half(xl, 1), :] = (sa[xrows_half(xl, 1), :] + ta_o[1].astype(F32)).astype(BF16)
    ta5 = send(sa16.at[xrows_half(xl, 1)], ta_r.at[hx:XB], xleft)
    tb0.wait_recv()
    sb16[yr, 0:hx, :] = (sb[yr, 0:hx, :] + tb_o[0].astype(F32)).astype(BF16)
    tb4 = send(sb16.at[yr, 0:hx], tb_l.at[0:hx], yright)
    tb1.wait_recv()
    sb16[yl, hx:XB, :] = (sb[yl, hx:XB, :] + tb_o[1].astype(F32)).astype(BF16)
    tb5 = send(sb16.at[yl, hx:XB], tb_r.at[hx:XB], yleft)

    for copy in (ta2, ta3, ta4, ta5):
        copy.wait_recv()
    tt[:, 0:Q] = sa[xrows(x), :] + ta_l[...].astype(F32) + ta_r[...].astype(F32)
    for copy in (tb2, tb3, tb4, tb5):
        copy.wait_recv()
    tt[:, Q:HALF] = sb[y] + tb_l[...].astype(F32) + tb_r[...].astype(F32)

    def part(zz, cc):
        return pl.ds(pl.multiple_of((zz * 2 + cc) * ROWS, 8), ROWS)

    for k in range(2):
        fz_send[k] = tt[part(1 - z, k), :].astype(BF16)
    f1 = send(fz_send.at[c], fz_recv.at[c], zsame)
    f2 = send(fz_send.at[1 - c], fz_recv.at[c], zother)
    fs_send[...] = tt[part(z, 1 - c), :]
    f0 = send(fs_send, fs_recv, sib)
    for copy in (f1, f2, f0):
        copy.wait_recv()
    wg_v[:, cols(c)] = (tt[part(z, c), :] + fz_recv[c].astype(F32)) * factor
    wg_v[:, cols(1 - c)] = (fs_recv[...] + fz_recv[1 - c].astype(F32)) * factor
    out0 = local(wg_v, wg_out)
    for copy in pending:
        copy.wait_send()
    for copy in (out0, out1, out2):
        copy.wait()


def shards(inner_input, inner_weight, grad_out, local_fragment, anchor, momentum):
    any_spec = pl.BlockSpec(memory_space=pl.ANY)
    vm = pltpu.VMEM
    hx = XB // 2
    wg, na, nm = pl.pallas_call(
        kernel,
        out_shape=(
            jax.ShapeDtypeStruct((ROWS, 1024), F32),
            jax.ShapeDtypeStruct((ROWS, WC), BF16),
            jax.ShapeDtypeStruct((ROWS, WC), F32),
        ),
        in_specs=[any_spec] * 6,
        out_specs=(any_spec,) * 3,
        scratch_shapes=[
            vm((2, TOK, D), BF16), vm((2, TOK, HALF), BF16), vm((2, 2, ROWS, HALF), BF16),
            vm((4, YB, Q), BF16), vm((4, YB, Q), BF16),
            vm((2, TOK, HALF), F32), vm((2, TOK, HALF), BF16),
            vm((4, YB, Q), BF16), vm((4, YB, Q), BF16),
            vm((2, YB // 2, Q), BF16), vm((YB, Q), BF16), vm((YB, Q), BF16),
            vm((2, 2, XB, Q), BF16), vm((4, XB, Q), BF16), vm((4, XB, Q), BF16),
            vm((YB, Q), F32), vm((4, XB, Q), F32), vm((YB, Q), BF16), vm((4, XB, Q), BF16),
            vm((2, hx, Q), BF16), vm((XB, Q), BF16), vm((XB, Q), BF16),
            vm((2, hx, Q), BF16), vm((XB, Q), BF16), vm((XB, Q), BF16),
            vm((XB, HALF), F32),
            vm((ROWS, HALF), F32), vm((ROWS, HALF), F32),
            vm((2, ROWS, HALF), BF16), vm((2, ROWS, HALF), BF16),
            vm((ROWS, 1024), F32),
            vm((4, ROWS, WC), BF16), vm((4, ROWS, WC), BF16), vm((ROWS, WC), F32),
            vm((4, 2, ROWS, WH), BF16),
            vm((2, ROWS, WH), BF16), vm((2, ROWS, WH), BF16), vm((2, ROWS, WH), BF16),
            vm((ROWS, WC), BF16), vm((ROWS, WC), F32),
            pltpu.SemaphoreType.DMA((16,)),
            pltpu.SemaphoreType.DMA((56,)),
            pltpu.SemaphoreType.DMA((56,)),
        ],
        compiler_params=pltpu.CompilerParams(
            collective_id=0, has_side_effects=True, vmem_limit_bytes=60 * 1024 * 1024
        ),
        cost_estimate=pl.CostEstimate(
            flops=4 * TOK * D * 1024, bytes_accessed=16 * 1024 * 1024, transcendentals=TOK * 1024
        ),
    )(inner_input[0], inner_weight[0], grad_out[0], local_fragment[0], anchor, momentum)
    return (wg[None], na, nm)


def solution(mesh):
    in_specs = (
        P("worker", "fsdp", None),
        P("worker", "fsdp", None),
        P("worker", "fsdp", None),
        P("worker", "fsdp", None),
        P("fsdp", None),
        P("fsdp", "worker"),
    )
    out_specs = (P("worker", "fsdp", None), P("fsdp", "worker"), P("fsdp", "worker"))
    return jax.shard_map(shards, mesh=mesh, in_specs=in_specs, out_specs=out_specs, check_vma=False)
```

```python
import jax
import jax.numpy as jnp
from jax import lax
from jax.experimental import pallas as pl
from jax.experimental.pallas import tpu as pltpu
from jax.sharding import PartitionSpec as P

F32 = jnp.float32
BF16 = jnp.bfloat16
MESH = pl.DeviceIdType.MESH

TOK = 512
D = 4608
HALF = 512
Q = 256
YB = 1152
XB = 288
ROWS = 72
WC = 4608
WH = 2304
SETS = 3


def ring(i):
    return lax.rem(i + 1, 4), lax.rem(i + 3, 4), lax.rem(i + 2, 4)


def step_of(top):
    q = top * (2.0**23 + 1.0)
    low = jnp.abs(q - q * (1.0 - 2.0**-24))
    return jnp.where(low < top, low * 0.5, low * 0.25)


def coded_of(delta, step):
    mag = jnp.abs(delta)
    level = jnp.where(mag >= 0.25 * step, 0.5, 0.0)
    level = jnp.where(mag >= 0.75 * step, 1.0, level)
    level = jnp.where(mag >= 1.25 * step, 1.5, level)
    level = jnp.where(mag >= 1.75 * step, 2.0, level)
    level = jnp.where(mag >= 2.5 * step, 3.0, level)
    level = jnp.where(mag >= 3.5 * step, 4.0, level)
    level = jnp.where(mag >= 5.0 * step, 6.0, level)
    coded = level * step
    return jnp.where(delta < 0, -coded, coded).astype(BF16)


def merge(a, b, bit, s):
    keep = jnp.where(bit, b, a)
    move = jnp.where(bit, pltpu.roll(b, s, 1), pltpu.roll(a, 128 - s, 1))
    return jnp.maximum(keep, move)


def code_chunk(delta_at, store):
    lane = lax.broadcasted_iota(jnp.int32, (ROWS, 128), 1)
    bit0, bit1, last = (lane & 1) == 1, (lane & 2) == 2, (lane & 28) == 28
    src = lax.broadcasted_iota(jnp.int32, (128, 512), 0)
    dst = lax.broadcasted_iota(jnp.int32, (128, 512), 1)
    spread = jnp.where(src == ((dst & 96) | 28 | (dst // 128)), 1.0, 0.0).astype(BF16)
    deltas, steps = [], []
    for k in range(SETS):
        four = [delta_at(4 * k + g) for g in range(4)]
        m = [jnp.abs(d) for d in four]
        top = merge(merge(m[0], m[1], bit0, 1), merge(m[2], m[3], bit0, 1), bit1, 2)
        for s in (4, 8, 16):
            top = jnp.maximum(top, pltpu.roll(top, s, 1))
        steps.append(jnp.where(last, step_of(top), 0.0))
        deltas.append(four)
    spread_steps = jnp.dot(
        jnp.concatenate(steps, axis=0).astype(BF16), spread, preferred_element_type=F32
    )
    for k in range(SETS):
        for g in range(4):
            step = spread_steps[ROWS * k:ROWS * (k + 1), 128 * g:128 * (g + 1)]
            store(4 * k + g, coded_of(deltas[k][g], step))


def kernel(
    x_in, w_in, g_in, loc_in, anc_in, mom_in,
    wg_out, na_out, nm_out,
    xs, gs, wraw, wa, wb, pre, act, pa, pb,
    ra_o, ra_l, ra_r, rb_o, rb_l, rb_r,
    sa, sb, sa16, sb16,
    ta_o, ta_l, ta_r, tb_o, tb_l, tb_r,
    tt, fs_send, fs_recv, fz_send, fz_recv, wg_v,
    loc, anc, mom, cod, wo, wl, wr, na_v, nm_v,
    lsem, ssem, rsem,
):
    me = lax.axis_index("fsdp")
    wk = lax.axis_index("worker")
    c = lax.rem(me, 2)
    z = lax.rem(me // 2, 2)
    x = lax.rem(me // 4, 4)
    y = me // 16
    xr, xl, xo = ring(x)
    yr, yl, yo = ring(y)
    wr_i, wl_i, wo_i = ring(wk)

    def dev(yy, xx, zz, cc):
        return (wk, ((yy * 4 + xx) * 2 + zz) * 2 + cc)

    sib = dev(y, x, z, 1 - c)
    zsame = dev(y, x, 1 - z, c)
    zother = dev(y, x, 1 - z, 1 - c)
    xright, xleft = dev(y, xr, z, c), dev(y, xl, z, c)
    yright, yleft = dev(yr, x, z, c), dev(yl, x, z, c)
    wright, wleft = (wr_i, me), (wl_i, me)

    pending = []
    count = [0]

    def send(src, dst, to):
        k = count[0]
        count[0] += 1
        copy = pltpu.make_async_remote_copy(
            src_ref=src, dst_ref=dst, send_sem=ssem.at[k], recv_sem=rsem.at[k],
            device_id=to, device_id_type=MESH,
        )
        copy.start()
        pending.append(copy)
        return copy

    lcount = [0]

    def local(src, dst):
        k = lcount[0]
        lcount[0] += 1
        copy = pltpu.make_async_copy(src, dst, lsem.at[k])
        copy.start()
        return copy

    def cols(j):
        return pl.ds(pl.multiple_of(j * HALF, HALF), HALF)

    def wcols(j):
        return pl.ds(pl.multiple_of(j * WC, 128), WC)

    def half(ref, h):
        return ref.at[:, h * WH:(h + 1) * WH]

    def xrows(j):
        return pl.ds(pl.multiple_of(j * XB, 16), XB)

    def xrows_half(j, h):
        return pl.ds(pl.multiple_of(j * XB + h * (XB // 2), 16), XB // 2)

    own_w = local(w_in.at[:, cols(c)], wraw.at[z, c])
    frag = {}
    for name, j in (("o", wo_i), ("r", wr_i), ("l", wl_i), ("s", wk)):
        frag[name] = (
            local(loc_in.at[:, wcols(j)], loc.at[j]),
            local(anc_in.at[:, wcols(j)], anc.at[j]),
        )
    own_x = local(x_in, xs.at[0])
    own_g = local(g_in.at[:, cols(c)], gs.at[0])
    own_m = local(mom_in, mom)

    barrier = pltpu.get_barrier_semaphore()
    partners = (sib, zsame, zother, xright, xleft, yright, yleft, wright, wleft)
    for p in partners:
        pl.semaphore_signal(barrier, inc=1, device_id=p, device_id_type=MESH)
    pl.semaphore_wait(barrier, len(partners))

    g1 = send(w_in.at[:, cols(c)], wraw.at[z, c], zsame)
    g2 = send(w_in.at[:, cols(1 - c)], wraw.at[z, c], zother)
    g0 = send(w_in.at[:, cols(1 - c)], wraw.at[z, c], sib)
    sx = send(x_in, xs.at[1], sib)
    sg = send(g_in.at[:, cols(1 - c)], gs.at[1], sib)

    def code_block(name, j):
        for copy in frag[name]:
            copy.wait()
        def body(i, carry):
            def at(g):
                return pl.ds(pl.multiple_of((i * (4 * SETS) + g) * 128, 128), 128)

            def delta_at(g):
                return anc[j, :, at(g)].astype(F32) - loc[j, :, at(g)].astype(F32)

            def store(g, value):
                cod[j, :, at(g)] = value

            code_chunk(delta_at, store)
            return carry
        lax.fori_loop(0, WC // (512 * SETS), body, 0)

    code_block("o", wo_i)
    w0 = send(half(cod.at[wo_i], 0), wo.at[0], wright)
    w1 = send(half(cod.at[wo_i], 1), wo.at[1], wleft)

    own_w.wait()
    for copy in (g1, g2, g0):
        copy.wait_recv()
    for zz in range(2):
        rows = jnp.concatenate(
            [wraw[zz, 0].astype(F32), wraw[zz, 1].astype(F32)], axis=0
        ).astype(BF16)
        wa[y, xrows_half(x, zz), :] = rows[:, :Q]
        wb[y, xrows_half(x, zz), :] = rows[:, Q:]

    a1 = send(wa.at[y, xrows(x)], wa.at[y, xrows(x)], xright)
    a2 = send(wa.at[y, xrows(x)], wa.at[y, xrows(x)], xleft)
    b1 = send(wb.at[y, xrows(x)], wb.at[y, xrows(x)], yright)
    b2 = send(wb.at[y, xrows(x)], wb.at[y, xrows(x)], yleft)

    code_block("r", wr_i)
    w2 = send(half(cod.at[wr_i], 1), half(wl, 1), wright)

    a1.wait_recv()
    a3 = send(wa.at[y, xrows_half(xl, 0)], wa.at[y, xrows_half(xl, 0)], xright)
    b1.wait_recv()
    b3 = send(wb.at[yl, xrows_half(x, 0)], wb.at[yl, xrows_half(x, 0)], yright)
    a2.wait_recv()
    a4 = send(wa.at[y, xrows_half(xr, 1)], wa.at[y, xrows_half(xr, 1)], xleft)
    b2.wait_recv()
    b4 = send(wb.at[yr, xrows_half(x, 1)], wb.at[yr, xrows_half(x, 1)], yleft)

    code_block("l", wl_i)
    w3 = send(half(cod.at[wl_i], 0), half(wr, 0), wleft)

    a3.wait_recv()
    a4.wait_recv()
    a5 = send(wa.at[y], wa.at[y], yright)
    a6 = send(wa.at[y], wa.at[y], yleft)
    b3.wait_recv()
    b4.wait_recv()
    b5 = send(wb.at[:, xrows(x)], wb.at[:, xrows(x)], xright)
    b6 = send(wb.at[:, xrows(x)], wb.at[:, xrows(x)], xleft)

    code_block("s", wk)

    def project(yy, first):
        def body(t, carry):
            lhs = xs[t, :, pl.ds(pl.multiple_of(yy * YB, 128), YB)]
            part = jnp.dot(lhs, wa[yy], preferred_element_type=F32)
            if first:
                pre[t, :, 0:Q] = part
            else:
                pre[t, :, 0:Q] += part
            return carry
        lax.fori_loop(0, 2, body, 0)

    def project_rest():
        def body(i, carry):
            t = i // 2
            r = pl.ds(pl.multiple_of(lax.rem(i, 2) * 256, 256), 256)
            pre[t, r, Q:HALF] = jnp.dot(
                xs[t, r, :], wb[...].reshape(D, Q), preferred_element_type=F32
            )
            return carry
        lax.fori_loop(0, 4, body, 0)

    own_x.wait()
    sx.wait_recv()
    project(y, True)

    a5.wait_recv()
    a7 = send(wa.at[yl, 0:YB // 2], wa.at[yl, 0:YB // 2], yright)
    a6.wait_recv()
    a8 = send(wa.at[yr, YB // 2:YB], wa.at[yr, YB // 2:YB], yleft)
    b5.wait_recv()
    b7 = send(wb.at[0:2, xrows(xl)], wb.at[0:2, xrows(xl)], xright)
    b6.wait_recv()
    b8 = send(wb.at[2:4, xrows(xr)], wb.at[2:4, xrows(xr)], xleft)

    w0.wait_recv()
    w1.wait_recv()
    for j, h in ((wr_i, 0), (wl_i, 1)):
        def body(i, carry, j=j, h=h):
            at = pl.ds(pl.multiple_of(i * 256, 256), 256)
            to = pl.ds(pl.multiple_of(h * WH + i * 256, 256), 256)
            cod[j, :, to] = (cod[j, :, to].astype(F32) + wo[h, :, at].astype(F32)).astype(BF16)
            return carry
        lax.fori_loop(0, WH // 256, body, 0)
    w4 = send(half(cod.at[wr_i], 0), half(wl, 0), wright)
    w5 = send(half(cod.at[wl_i], 1), half(wr, 1), wleft)

    project(yl, False)
    project(yr, False)
    a7.wait_recv()
    a8.wait_recv()
    project(yo, False)
    b7.wait_recv()
    b8.wait_recv()
    project_rest()

    own_g.wait()
    sg.wait_recv()
    factor = D ** (-0.5)

    def activate(i, carry):
        t = i // 8
        r = pl.ds(pl.multiple_of(lax.rem(i, 8) * 64, 64), 64)
        value = pre[t, r, :] * factor
        sig = jax.nn.sigmoid(value)
        act[t, r, :] = (gs[t, r, :].astype(F32) * sig * (1.0 + value * (1.0 - sig))).astype(BF16)
        return carry

    lax.fori_loop(0, 16, activate, 0)

    def backward(yy, out, col):
        at = pl.ds(pl.multiple_of(yy * YB, 128), YB)
        dims = (((0,), (0,)), ((), ()))
        part = lax.dot_general(xs[0, :, at], act[0, :, col:col + Q], dims, preferred_element_type=F32)
        part += lax.dot_general(xs[1, :, at], act[1, :, col:col + Q], dims, preferred_element_type=F32)
        out[yy] = part.astype(BF16)

    hy = YB // 2
    backward(yo, pa, 0)
    ra0 = send(pa.at[yo, 0:hy], ra_o.at[0], yright)
    ra1 = send(pa.at[yo, hy:YB], ra_o.at[1], yleft)
    backward(yr, pa, 0)
    ra2 = send(pa.at[yr, hy:YB], ra_l.at[hy:YB], yright)
    backward(yl, pa, 0)
    ra3 = send(pa.at[yl, 0:hy], ra_r.at[0:hy], yleft)

    def backward_rest(yy, carry):
        backward(yy, pb, Q)
        return carry

    lax.fori_loop(0, 4, backward_rest, 0)
    rb0 = send(pb.at[0:2, xrows(xo)], rb_o.at[0], xright)
    rb1 = send(pb.at[2:4, xrows(xo)], rb_o.at[1], xleft)
    rb2 = send(pb.at[2:4, xrows(xr)], rb_l.at[2:4], xright)
    rb3 = send(pb.at[0:2, xrows(xl)], rb_r.at[0:2], xleft)
    backward(y, pa, 0)

    def add_rows(dst, at, other, n):
        def body(i, carry):
            r = pl.ds(pl.multiple_of(i * 96, 16), 96)
            d = pl.ds(pl.multiple_of(at[1] + i * 96, 16), 96)
            dst[at[0], d, :] = (dst[at[0], d, :].astype(F32) + other(r).astype(F32)).astype(BF16)
            return carry
        lax.fori_loop(0, n // 96, body, 0)

    ra0.wait_recv()
    add_rows(pa, (yr, 0), lambda r: ra_o[0, r, :], hy)
    ra4 = send(pa.at[yr, 0:hy], ra_l.at[0:hy], yright)
    ra1.wait_recv()
    add_rows(pa, (yl, hy), lambda r: ra_o[1, r, :], hy)
    ra5 = send(pa.at[yl, hy:YB], ra_r.at[hy:YB], yleft)
    rb0.wait_recv()
    for k in range(2):
        add_rows(pb, (k, xr * XB), lambda r, k=k: rb_o[0, k, r, :], XB)
    rb4 = send(pb.at[0:2, xrows(xr)], rb_l.at[0:2], xright)
    rb1.wait_recv()
    for k in range(2):
        add_rows(pb, (2 + k, xl * XB), lambda r, k=k: rb_o[1, k, r, :], XB)
    rb5 = send(pb.at[2:4, xrows(xl)], rb_r.at[2:4], xleft)

    for copy in (w2, w3, w4, w5):
        copy.wait_recv()
    own_m.wait()

    def outer(i, carry):
        at = pl.ds(pl.multiple_of(i * 256, 256), 256)
        total = cod[wk, :, at].astype(F32) + wl[:, at].astype(F32) + wr[:, at].astype(F32)
        grad = total * 0.25
        fresh = 0.9 * mom[:, at] + grad
        nm_v[:, at] = fresh
        na_v[:, at] = (anc[wk, :, at].astype(F32) - 0.7 * (grad + 0.9 * fresh)).astype(BF16)
        return carry

    lax.fori_loop(0, WC // 256, outer, 0)
    out1 = local(na_v, na_out)
    out2 = local(nm_v, nm_out)

    for copy in (ra2, ra3, ra4, ra5):
        copy.wait_recv()

    def sum_a(i, carry):
        r = pl.ds(pl.multiple_of(i * 96, 96), 96)
        total = pa[y, r, :].astype(F32) + ra_l[r, :].astype(F32) + ra_r[r, :].astype(F32)
        sa[r, :] = total
        sa16[r, :] = total.astype(BF16)
        return carry

    lax.fori_loop(0, YB // 96, sum_a, 0)
    hx = XB // 2
    ta0 = send(sa16.at[xrows_half(xo, 0)], ta_o.at[0], xright)
    ta1 = send(sa16.at[xrows_half(xo, 1)], ta_o.at[1], xleft)
    ta2 = send(sa16.at[xrows_half(xr, 1)], ta_l.at[hx:XB], xright)
    ta3 = send(sa16.at[xrows_half(xl, 0)], ta_r.at[0:hx], xleft)

    for copy in (rb2, rb3, rb4, rb5):
        copy.wait_recv()

    def sum_b(i, carry):
        k = i // 3
        r = pl.ds(pl.multiple_of(lax.rem(i, 3) * 96, 96), 96)
        at = pl.ds(pl.multiple_of(x * XB + lax.rem(i, 3) * 96, 16), 96)
        total = pb[k, at, :].astype(F32) + rb_l[k, r, :].astype(F32) + rb_r[k, r, :].astype(F32)
        sb[k, r, :] = total
        sb16[k, r, :] = total.astype(BF16)
        return carry

    lax.fori_loop(0, 12, sum_b, 0)
    tb0 = send(sb16.at[yo, 0:hx], tb_o.at[0], yright)
    tb1 = send(sb16.at[yo, hx:XB], tb_o.at[1], yleft)
    tb2 = send(sb16.at[yr, hx:XB], tb_l.at[hx:XB], yright)
    tb3 = send(sb16.at[yl, 0:hx], tb_r.at[0:hx], yleft)

    ta0.wait_recv()
    sa16[xrows_half(xr, 0), :] = (sa[xrows_half(xr, 0), :] + ta_o[0].astype(F32)).astype(BF16)
    ta4 = send(sa16.at[xrows_half(xr, 0)], ta_l.at[0:hx], xright)
    ta1.wait_recv()
    sa16[xrows_half(xl, 1), :] = (sa[xrows_half(xl, 1), :] + ta_o[1].astype(F32)).astype(BF16)
    ta5 = send(sa16.at[xrows_half(xl, 1)], ta_r.at[hx:XB], xleft)
    tb0.wait_recv()
    sb16[yr, 0:hx, :] = (sb[yr, 0:hx, :] + tb_o[0].astype(F32)).astype(BF16)
    tb4 = send(sb16.at[yr, 0:hx], tb_l.at[0:hx], yright)
    tb1.wait_recv()
    sb16[yl, hx:XB, :] = (sb[yl, hx:XB, :] + tb_o[1].astype(F32)).astype(BF16)
    tb5 = send(sb16.at[yl, hx:XB], tb_r.at[hx:XB], yleft)

    for copy in (ta2, ta3, ta4, ta5):
        copy.wait_recv()
    tt[:, 0:Q] = sa[xrows(x), :] + ta_l[...].astype(F32) + ta_r[...].astype(F32)
    for copy in (tb2, tb3, tb4, tb5):
        copy.wait_recv()
    tt[:, Q:HALF] = sb[y] + tb_l[...].astype(F32) + tb_r[...].astype(F32)

    def part(zz, cc):
        return pl.ds(pl.multiple_of((zz * 2 + cc) * ROWS, 8), ROWS)

    for k in range(2):
        fz_send[k] = tt[part(1 - z, k), :].astype(BF16)
    f1 = send(fz_send.at[c], fz_recv.at[c], zsame)
    f2 = send(fz_send.at[1 - c], fz_recv.at[c], zother)
    fs_send[...] = tt[part(z, 1 - c), :]
    f0 = send(fs_send, fs_recv, sib)
    for copy in (f1, f2, f0):
        copy.wait_recv()
    wg_v[:, cols(c)] = (tt[part(z, c), :] + fz_recv[c].astype(F32)) * factor
    wg_v[:, cols(1 - c)] = (fs_recv[...] + fz_recv[1 - c].astype(F32)) * factor
    out0 = local(wg_v, wg_out)
    for copy in pending:
        copy.wait_send()
    for copy in (out0, out1, out2):
        copy.wait()


def shards(inner_input, inner_weight, grad_out, local_fragment, anchor, momentum):
    any_spec = pl.BlockSpec(memory_space=pl.ANY)
    vm = pltpu.VMEM
    hx = XB // 2
    wg, na, nm = pl.pallas_call(
        kernel,
        out_shape=(
            jax.ShapeDtypeStruct((ROWS, 1024), F32),
            jax.ShapeDtypeStruct((ROWS, WC), BF16),
            jax.ShapeDtypeStruct((ROWS, WC), F32),
        ),
        in_specs=[any_spec] * 6,
        out_specs=(any_spec,) * 3,
        scratch_shapes=[
            vm((2, TOK, D), BF16), vm((2, TOK, HALF), BF16), vm((2, 2, ROWS, HALF), BF16),
            vm((4, YB, Q), BF16), vm((4, YB, Q), BF16),
            vm((2, TOK, HALF), F32), vm((2, TOK, HALF), BF16),
            vm((4, YB, Q), BF16), vm((4, YB, Q), BF16),
            vm((2, YB // 2, Q), BF16), vm((YB, Q), BF16), vm((YB, Q), BF16),
            vm((2, 2, XB, Q), BF16), vm((4, XB, Q), BF16), vm((4, XB, Q), BF16),
            vm((YB, Q), F32), vm((4, XB, Q), F32), vm((YB, Q), BF16), vm((4, XB, Q), BF16),
            vm((2, hx, Q), BF16), vm((XB, Q), BF16), vm((XB, Q), BF16),
            vm((2, hx, Q), BF16), vm((XB, Q), BF16), vm((XB, Q), BF16),
            vm((XB, HALF), F32),
            vm((ROWS, HALF), F32), vm((ROWS, HALF), F32),
            vm((2, ROWS, HALF), BF16), vm((2, ROWS, HALF), BF16),
            vm((ROWS, 1024), F32),
            vm((4, ROWS, WC), BF16), vm((4, ROWS, WC), BF16), vm((ROWS, WC), F32),
            vm((4, ROWS, WC), BF16),
            vm((2, ROWS, WH), BF16), vm((ROWS, WC), BF16), vm((ROWS, WC), BF16),
            vm((ROWS, WC), BF16), vm((ROWS, WC), F32),
            pltpu.SemaphoreType.DMA((16,)),
            pltpu.SemaphoreType.DMA((56,)),
            pltpu.SemaphoreType.DMA((56,)),
        ],
        compiler_params=pltpu.CompilerParams(
            collective_id=0, has_side_effects=True, vmem_limit_bytes=60 * 1024 * 1024
        ),
        cost_estimate=pl.CostEstimate(
            flops=4 * TOK * D * 1024, bytes_accessed=16 * 1024 * 1024, transcendentals=TOK * 1024
        ),
    )(inner_input[0], inner_weight[0], grad_out[0], local_fragment[0], anchor, momentum)
    return (wg[None], na, nm)


def solution(mesh):
    in_specs = (
        P("worker", "fsdp", None),
        P("worker", "fsdp", None),
        P("worker", "fsdp", None),
        P("worker", "fsdp", None),
        P("fsdp", None),
        P("fsdp", "worker"),
    )
    out_specs = (P("worker", "fsdp", None), P("fsdp", "worker"), P("fsdp", "worker"))
    return jax.shard_map(shards, mesh=mesh, in_specs=in_specs, out_specs=out_specs, check_vma=False)
```

```python
import jax
import jax.numpy as jnp
from jax import lax
from jax.experimental import pallas as pl
from jax.experimental.pallas import tpu as pltpu
from jax.sharding import PartitionSpec as P

F32 = jnp.float32
BF16 = jnp.bfloat16
MESH = pl.DeviceIdType.MESH

TOK = 512
D = 4608
HALF = 512
R = 128
YB = 1152
XB = 288
ROWS = 72
WC = 4608
WH = 2304
SETS = 3


def ring(i):
    return lax.rem(i + 1, 4), lax.rem(i + 3, 4), lax.rem(i + 2, 4)


def step_of(top):
    q = top * (2.0**23 + 1.0)
    low = jnp.abs(q - q * (1.0 - 2.0**-24))
    return jnp.where(low < top, low * 0.5, low * 0.25)


def coded_of(delta, step):
    mag = jnp.abs(delta)
    level = jnp.where(mag >= 0.25 * step, 0.5, 0.0)
    level = jnp.where(mag >= 0.75 * step, 1.0, level)
    level = jnp.where(mag >= 1.25 * step, 1.5, level)
    level = jnp.where(mag >= 1.75 * step, 2.0, level)
    level = jnp.where(mag >= 2.5 * step, 3.0, level)
    level = jnp.where(mag >= 3.5 * step, 4.0, level)
    level = jnp.where(mag >= 5.0 * step, 6.0, level)
    coded = level * step
    return jnp.where(delta < 0, -coded, coded).astype(BF16)


def merge(a, b, bit, s):
    keep = jnp.where(bit, b, a)
    move = jnp.where(bit, pltpu.roll(b, s, 1), pltpu.roll(a, 128 - s, 1))
    return jnp.maximum(keep, move)


def code_chunk(delta_at, store):
    lane = lax.broadcasted_iota(jnp.int32, (ROWS, 128), 1)
    bit0, bit1, last = (lane & 1) == 1, (lane & 2) == 2, (lane & 28) == 28
    src = lax.broadcasted_iota(jnp.int32, (128, 512), 0)
    dst = lax.broadcasted_iota(jnp.int32, (128, 512), 1)
    spread = jnp.where(src == ((dst & 96) | 28 | (dst // 128)), 1.0, 0.0).astype(BF16)
    deltas, steps = [], []
    for k in range(SETS):
        four = [delta_at(4 * k + g) for g in range(4)]
        m = [jnp.abs(d) for d in four]
        top = merge(merge(m[0], m[1], bit0, 1), merge(m[2], m[3], bit0, 1), bit1, 2)
        for s in (4, 8, 16):
            top = jnp.maximum(top, pltpu.roll(top, s, 1))
        steps.append(jnp.where(last, step_of(top), 0.0))
        deltas.append(four)
    spread_steps = jnp.dot(
        jnp.concatenate(steps, axis=0).astype(BF16), spread, preferred_element_type=F32
    )
    for k in range(SETS):
        for g in range(4):
            step = spread_steps[ROWS * k:ROWS * (k + 1), 128 * g:128 * (g + 1)]
            store(4 * k + g, coded_of(deltas[k][g], step))


def kernel(
    x_in, w_in, g_in, loc_in, anc_in, mom_in,
    wg_out, na_out, nm_out,
    xs, gs, wraw, wa, wb, act, pa, pb,
    ra_o, ra_l, ra_r, rb_o, rb_l, rb_r,
    sa, sb, sa16, sb16,
    ta_o, ta_l, ta_r, tb_o, tb_l, tb_r,
    tt, fs_send, fs_recv, fz_send, fz_recv, wg_v,
    loc, anc, mom, cod, wo, wl, wr, na_v, nm_v,
    lsem, ssem, rsem,
):
    me = lax.axis_index("fsdp")
    wk = lax.axis_index("worker")
    c = lax.rem(me, 2)
    z = lax.rem(me // 2, 2)
    x = lax.rem(me // 4, 4)
    y = me // 16
    xr, xl, xo = ring(x)
    yr, yl, yo = ring(y)
    wr_i, wl_i, wo_i = ring(wk)
    hy, hx = YB // 2, XB // 2
    factor = D ** (-0.5)

    def dev(yy, xx, zz, cc):
        return (wk, ((yy * 4 + xx) * 2 + zz) * 2 + cc)

    sib = dev(y, x, z, 1 - c)
    zsame = dev(y, x, 1 - z, c)
    zother = dev(y, x, 1 - z, 1 - c)
    xright, xleft = dev(y, xr, z, c), dev(y, xl, z, c)
    yright, yleft = dev(yr, x, z, c), dev(yl, x, z, c)
    wright, wleft = (wr_i, me), (wl_i, me)

    pending = []

    def send(src, dst, to):
        k = len(pending)
        copy = pltpu.make_async_remote_copy(
            src_ref=src, dst_ref=dst, send_sem=ssem.at[k], recv_sem=rsem.at[k],
            device_id=to, device_id_type=MESH,
        )
        copy.start()
        pending.append(copy)
        return copy

    started = []

    def local(src, dst):
        copy = pltpu.make_async_copy(src, dst, lsem.at[len(started)])
        copy.start()
        started.append(copy)
        return copy

    def arrived(*copies):
        for copy in copies:
            copy.wait_recv()

    def cols(j):
        return pl.ds(pl.multiple_of(j * HALF, HALF), HALF)

    def wcols(j):
        return pl.ds(pl.multiple_of(j * WC, 128), WC)

    def half(ref, h):
        return ref.at[:, h * WH:(h + 1) * WH]

    def xrows(j):
        return pl.ds(pl.multiple_of(j * XB, 16), XB)

    def xrows_half(j, h):
        return pl.ds(pl.multiple_of(j * XB + h * hx, 16), hx)

    own_w = local(w_in.at[:, cols(c)], wraw.at[z, c])
    frag = {}
    for name, j in (("o", wo_i), ("r", wr_i), ("l", wl_i), ("s", wk)):
        frag[name] = (
            local(loc_in.at[:, wcols(j)], loc.at[j]),
            local(anc_in.at[:, wcols(j)], anc.at[j]),
        )
    own_x = local(x_in, xs.at[0])
    own_g = local(g_in.at[:, cols(c)], gs.at[0])
    own_m = local(mom_in, mom)

    barrier = pltpu.get_barrier_semaphore()
    partners = (sib, zsame, zother, xright, xleft, yright, yleft, wright, wleft)
    for p in partners:
        pl.semaphore_signal(barrier, inc=1, device_id=p, device_id_type=MESH)
    pl.semaphore_wait(barrier, len(partners))

    g1 = send(w_in.at[:, cols(c)], wraw.at[z, c], zsame)
    g2 = send(w_in.at[:, cols(1 - c)], wraw.at[z, c], zother)
    g0 = send(w_in.at[:, cols(1 - c)], wraw.at[z, c], sib)

    def code_block(name, j):
        for copy in frag[name]:
            copy.wait()

        def body(i, carry):
            def at(g):
                return pl.ds(pl.multiple_of((i * (4 * SETS) + g) * 128, 128), 128)

            def delta_at(g):
                return anc[j, :, at(g)].astype(F32) - loc[j, :, at(g)].astype(F32)

            def store(g, value):
                cod[j, :, at(g)] = value

            code_chunk(delta_at, store)
            return carry

        lax.fori_loop(0, WC // (512 * SETS), body, 0)

    state = [{}, {}]

    def gather1(s):
        st = state[s]
        mine_a, mine_b = wa.at[s, y, xrows(x)], wb.at[s, y, xrows(x)]
        st["g1"] = (
            send(mine_a, mine_a, xright), send(mine_b, mine_b, yright),
            send(mine_a, mine_a, xleft), send(mine_b, mine_b, yleft),
        )

    def gather1_next(s):
        st = state[s]
        steps = (
            (wa.at[s, y, xrows_half(xl, 0)], xright), (wb.at[s, yl, xrows_half(x, 0)], yright),
            (wa.at[s, y, xrows_half(xr, 1)], xleft), (wb.at[s, yr, xrows_half(x, 1)], yleft),
        )
        out = []
        for copy, (ref, to) in zip(st["g1"], steps):
            arrived(copy)
            out.append(send(ref, ref, to))
        st["g2"] = out

    def gather2(s):
        st = state[s]
        a_r, b_r, a_l, b_l = st["g2"]
        arrived(a_r, a_l)
        mine_a, mine_b = wa.at[s, y], wb.at[s, :, xrows(x)]
        a_r, a_l = send(mine_a, mine_a, yright), send(mine_a, mine_a, yleft)
        arrived(b_r, b_l)
        b_r, b_l = send(mine_b, mine_b, xright), send(mine_b, mine_b, xleft)
        st["g3"] = (a_r, b_r, a_l, b_l)

    def gather2_next(s):
        st = state[s]
        steps = (
            (wa.at[s, yl, 0:hy], yright), (wb.at[s, 0:2, xrows(xl)], xright),
            (wa.at[s, yr, hy:YB], yleft), (wb.at[s, 2:4, xrows(xr)], xleft),
        )
        out = []
        for copy, (ref, to) in zip(st["g3"], steps):
            arrived(copy)
            out.append(send(ref, ref, to))
        st["g4"] = out

    def forward(s):
        arrived(*state[s]["g4"])

        def body(i, carry):
            t = i // 2
            r = pl.ds(pl.multiple_of(lax.rem(i, 2) * 256, 256), 256)
            weight = jnp.concatenate([wa[s].reshape(D, R), wb[s].reshape(D, R)], axis=1)
            value = jnp.dot(xs[t, r, :], weight, preferred_element_type=F32) * factor
            sig = jax.nn.sigmoid(value)
            cot = gs[t, r, 2 * R * s:2 * R * (s + 1)].astype(F32)
            act[s, t, r, :] = (cot * sig * (1.0 + value * (1.0 - sig))).astype(BF16)
            return carry

        lax.fori_loop(0, 4, body, 0)

    def backward(s, yy):
        at = pl.ds(pl.multiple_of(yy * YB, 128), YB)
        dims = (((0,), (0,)), ((), ()))
        part = lax.dot_general(xs[0, :, at], act[s, 0], dims, preferred_element_type=F32)
        part += lax.dot_general(xs[1, :, at], act[s, 1], dims, preferred_element_type=F32)
        pa[s, yy] = part[:, :R].astype(BF16)
        pb[s, yy] = part[:, R:].astype(BF16)

    def reduce1(s):
        st = state[s]
        backward(s, yo)
        a0 = send(pa.at[s, yo, 0:hy], ra_o.at[s, 0], yright)
        a1 = send(pa.at[s, yo, hy:YB], ra_o.at[s, 1], yleft)
        backward(s, yr)
        a2 = send(pa.at[s, yr, hy:YB], ra_l.at[s, hy:YB], yright)
        backward(s, yl)
        a3 = send(pa.at[s, yl, 0:hy], ra_r.at[s, 0:hy], yleft)
        backward(s, y)
        b0 = send(pb.at[s, 0:2, xrows(xo)], rb_o.at[s, 0], xright)
        b1 = send(pb.at[s, 2:4, xrows(xo)], rb_o.at[s, 1], xleft)
        b2 = send(pb.at[s, 2:4, xrows(xr)], rb_l.at[s, 2:4], xright)
        b3 = send(pb.at[s, 0:2, xrows(xl)], rb_r.at[s, 0:2], xleft)
        st["r1"] = (a0, a1, b0, b1)
        st["ra"], st["rb"] = [a2, a3], [b2, b3]

    def add_to(dst, at, other, n):
        def body(i, carry):
            r = pl.ds(pl.multiple_of(i * 96, 16), 96)
            d = pl.ds(pl.multiple_of(at + i * 96, 16), 96)
            dst[d, :] = (dst[d, :].astype(F32) + other[r, :].astype(F32)).astype(BF16)
            return carry

        lax.fori_loop(0, n // 96, body, 0)

    def reduce1_next(s):
        st = state[s]
        a0, a1, b0, b1 = st["r1"]
        arrived(a0)
        add_to(pa.at[s, yr], 0, ra_o.at[s, 0], hy)
        st["ra"].append(send(pa.at[s, yr, 0:hy], ra_l.at[s, 0:hy], yright))
        arrived(a1)
        add_to(pa.at[s, yl], hy, ra_o.at[s, 1], hy)
        st["ra"].append(send(pa.at[s, yl, hy:YB], ra_r.at[s, hy:YB], yleft))
        arrived(b0)
        for k in range(2):
            add_to(pb.at[s, k], xr * XB, rb_o.at[s, 0, k], XB)
        st["rb"].append(send(pb.at[s, 0:2, xrows(xr)], rb_l.at[s, 0:2], xright))
        arrived(b1)
        for k in range(2):
            add_to(pb.at[s, 2 + k], xl * XB, rb_o.at[s, 1, k], XB)
        st["rb"].append(send(pb.at[s, 2:4, xrows(xl)], rb_r.at[s, 2:4], xleft))

    def reduce2(s):
        st = state[s]
        arrived(*st["ra"])

        def sum_a(i, carry):
            r = pl.ds(pl.multiple_of(i * 192, 96), 192)
            total = pa[s, y, r, :].astype(F32) + ra_l[s, r, :].astype(F32) + ra_r[s, r, :].astype(F32)
            sa[s, r, :] = total
            sa16[s, r, :] = total.astype(BF16)
            return carry

        lax.fori_loop(0, YB // 192, sum_a, 0)
        a0 = send(sa16.at[s, xrows_half(xo, 0)], ta_o.at[s, 0], xright)
        a1 = send(sa16.at[s, xrows_half(xo, 1)], ta_o.at[s, 1], xleft)
        a2 = send(sa16.at[s, xrows_half(xr, 1)], ta_l.at[s, hx:XB], xright)
        a3 = send(sa16.at[s, xrows_half(xl, 0)], ta_r.at[s, 0:hx], xleft)

        arrived(*st["rb"])

        def sum_b(k, carry):
            total = pb[s, k, xrows(x), :].astype(F32) + rb_l[s, k].astype(F32) + rb_r[s, k].astype(F32)
            sb[s, k] = total
            sb16[s, k] = total.astype(BF16)
            return carry

        lax.fori_loop(0, 4, sum_b, 0)
        b0 = send(sb16.at[s, yo, 0:hx], tb_o.at[s, 0], yright)
        b1 = send(sb16.at[s, yo, hx:XB], tb_o.at[s, 1], yleft)
        b2 = send(sb16.at[s, yr, hx:XB], tb_l.at[s, hx:XB], yright)
        b3 = send(sb16.at[s, yl, 0:hx], tb_r.at[s, 0:hx], yleft)
        st["t1"] = (a0, a1, b0, b1)
        st["ta"], st["tb"] = [a2, a3], [b2, b3]

    def reduce2_next(s):
        st = state[s]
        a0, a1, b0, b1 = st["t1"]
        arrived(a0)
        r = xrows_half(xr, 0)
        sa16[s, r, :] = (sa[s, r, :] + ta_o[s, 0].astype(F32)).astype(BF16)
        st["ta"].append(send(sa16.at[s, r], ta_l.at[s, 0:hx], xright))
        arrived(a1)
        r = xrows_half(xl, 1)
        sa16[s, r, :] = (sa[s, r, :] + ta_o[s, 1].astype(F32)).astype(BF16)
        st["ta"].append(send(sa16.at[s, r], ta_r.at[s, hx:XB], xleft))
        arrived(b0)
        sb16[s, yr, 0:hx, :] = (sb[s, yr, 0:hx, :] + tb_o[s, 0].astype(F32)).astype(BF16)
        st["tb"].append(send(sb16.at[s, yr, 0:hx], tb_l.at[s, 0:hx], yright))
        arrived(b1)
        sb16[s, yl, hx:XB, :] = (sb[s, yl, hx:XB, :] + tb_o[s, 1].astype(F32)).astype(BF16)
        st["tb"].append(send(sb16.at[s, yl, hx:XB], tb_r.at[s, hx:XB], yleft))

    def part(zz, cc):
        return pl.ds(pl.multiple_of((zz * 2 + cc) * ROWS, 8), ROWS)

    def reduce3(s):
        st = state[s]
        arrived(*st["ta"])
        tt[s, :, 0:R] = sa[s, xrows(x), :] + ta_l[s].astype(F32) + ta_r[s].astype(F32)
        arrived(*st["tb"])
        tt[s, :, R:2 * R] = sb[s, y] + tb_l[s].astype(F32) + tb_r[s].astype(F32)
        for k in range(2):
            fz_send[s, k] = tt[s, part(1 - z, k), :].astype(BF16)
        f1 = send(fz_send.at[s, c], fz_recv.at[s, c], zsame)
        f2 = send(fz_send.at[s, 1 - c], fz_recv.at[s, c], zother)
        fs_send[s] = tt[s, part(z, 1 - c), :]
        f0 = send(fs_send.at[s], fs_recv.at[s], sib)
        st["f"] = (f1, f2, f0)

    def last(s):
        arrived(*state[s]["f"])

        def at(j):
            return pl.ds(pl.multiple_of(j * HALF + 2 * R * s, 2 * R), 2 * R)

        wg_v[:, at(c)] = (tt[s, part(z, c), :] + fz_recv[s, c].astype(F32)) * factor
        wg_v[:, at(1 - c)] = (fs_recv[s] + fz_recv[s, 1 - c].astype(F32)) * factor

    code_block("o", wo_i)
    w0 = send(half(cod.at[wo_i], 0), wo.at[0], wright)
    w1 = send(half(cod.at[wo_i], 1), wo.at[1], wleft)

    own_w.wait()
    arrived(g1, g2, g0)
    for zz in range(2):
        rows = jnp.concatenate(
            [wraw[zz, 0].astype(F32), wraw[zz, 1].astype(F32)], axis=0
        ).astype(BF16)
        for s in range(2):
            wa[s, y, xrows_half(x, zz), :] = rows[:, 2 * R * s:2 * R * s + R]
            wb[s, y, xrows_half(x, zz), :] = rows[:, 2 * R * s + R:2 * R * (s + 1)]

    gather1(0)
    sx = send(x_in, xs.at[1], sib)
    sg = send(g_in.at[:, cols(1 - c)], gs.at[1], sib)

    code_block("r", wr_i)
    w2 = send(half(cod.at[wr_i], 1), half(wl, 1), wright)
    gather1_next(0)
    gather1(1)
    code_block("l", wl_i)
    w3 = send(half(cod.at[wl_i], 0), half(wr, 0), wleft)
    gather2(0)
    gather1_next(1)
    code_block("s", wk)
    gather2_next(0)
    gather2(1)

    arrived(w0, w1)
    for j, h in ((wr_i, 0), (wl_i, 1)):
        def body(i, carry, j=j, h=h):
            at = pl.ds(pl.multiple_of(i * 256, 256), 256)
            to = pl.ds(pl.multiple_of(h * WH + i * 256, 256), 256)
            cod[j, :, to] = (cod[j, :, to].astype(F32) + wo[h, :, at].astype(F32)).astype(BF16)
            return carry
        lax.fori_loop(0, WH // 256, body, 0)
    w4 = send(half(cod.at[wr_i], 0), half(wl, 0), wright)
    w5 = send(half(cod.at[wl_i], 1), half(wr, 1), wleft)

    own_x.wait()
    own_g.wait()
    arrived(sx, sg)
    forward(0)
    gather2_next(1)
    reduce1(0)
    forward(1)
    reduce1_next(0)
    reduce1(1)
    reduce2(0)
    reduce1_next(1)

    arrived(w2, w3, w4, w5)
    own_m.wait()

    def outer(i, carry):
        at = pl.ds(pl.multiple_of(i * 256, 256), 256)
        total = cod[wk, :, at].astype(F32) + wl[:, at].astype(F32) + wr[:, at].astype(F32)
        grad = total * 0.25
        fresh = 0.9 * mom[:, at] + grad
        nm_v[:, at] = fresh
        na_v[:, at] = (anc[wk, :, at].astype(F32) - 0.7 * (grad + 0.9 * fresh)).astype(BF16)
        return carry

    lax.fori_loop(0, WC // 256, outer, 0)
    out1 = local(na_v, na_out)
    out2 = local(nm_v, nm_out)

    reduce2_next(0)
    reduce2(1)
    reduce3(0)
    reduce2_next(1)
    reduce3(1)
    last(0)
    last(1)
    out0 = local(wg_v, wg_out)
    for copy in pending:
        copy.wait_send()
    for copy in (out0, out1, out2):
        copy.wait()


def shards(inner_input, inner_weight, grad_out, local_fragment, anchor, momentum):
    any_spec = pl.BlockSpec(memory_space=pl.ANY)
    vm = pltpu.VMEM
    hy, hx = YB // 2, XB // 2
    wg, na, nm = pl.pallas_call(
        kernel,
        out_shape=(
            jax.ShapeDtypeStruct((ROWS, 1024), F32),
            jax.ShapeDtypeStruct((ROWS, WC), BF16),
            jax.ShapeDtypeStruct((ROWS, WC), F32),
        ),
        in_specs=[any_spec] * 6,
        out_specs=(any_spec,) * 3,
        scratch_shapes=[
            vm((2, TOK, D), BF16), vm((2, TOK, HALF), BF16), vm((2, 2, ROWS, HALF), BF16),
            vm((2, 4, YB, R), BF16), vm((2, 4, YB, R), BF16),
            vm((2, 2, TOK, 2 * R), BF16),
            vm((2, 4, YB, R), BF16), vm((2, 4, YB, R), BF16),
            vm((2, 2, hy, R), BF16), vm((2, YB, R), BF16), vm((2, YB, R), BF16),
            vm((2, 2, 2, XB, R), BF16), vm((2, 4, XB, R), BF16), vm((2, 4, XB, R), BF16),
            vm((2, YB, R), F32), vm((2, 4, XB, R), F32), vm((2, YB, R), BF16), vm((2, 4, XB, R), BF16),
            vm((2, 2, hx, R), BF16), vm((2, XB, R), BF16), vm((2, XB, R), BF16),
            vm((2, 2, hx, R), BF16), vm((2, XB, R), BF16), vm((2, XB, R), BF16),
            vm((2, XB, 2 * R), F32),
            vm((2, ROWS, 2 * R), F32), vm((2, ROWS, 2 * R), F32),
            vm((2, 2, ROWS, 2 * R), BF16), vm((2, 2, ROWS, 2 * R), BF16),
            vm((ROWS, 1024), F32),
            vm((4, ROWS, WC), BF16), vm((4, ROWS, WC), BF16), vm((ROWS, WC), F32),
            vm((4, ROWS, WC), BF16),
            vm((2, ROWS, WH), BF16), vm((ROWS, WC), BF16), vm((ROWS, WC), BF16),
            vm((ROWS, WC), BF16), vm((ROWS, WC), F32),
            pltpu.SemaphoreType.DMA((16,)),
            pltpu.SemaphoreType.DMA((100,)),
            pltpu.SemaphoreType.DMA((100,)),
        ],
        compiler_params=pltpu.CompilerParams(
            collective_id=0, has_side_effects=True, vmem_limit_bytes=60 * 1024 * 1024
        ),
        cost_estimate=pl.CostEstimate(
            flops=4 * TOK * D * 1024, bytes_accessed=16 * 1024 * 1024, transcendentals=TOK * 1024
        ),
    )(inner_input[0], inner_weight[0], grad_out[0], local_fragment[0], anchor, momentum)
    return (wg[None], na, nm)


def solution(mesh):
    in_specs = (
        P("worker", "fsdp", None),
        P("worker", "fsdp", None),
        P("worker", "fsdp", None),
        P("worker", "fsdp", None),
        P("fsdp", None),
        P("fsdp", "worker"),
    )
    out_specs = (P("worker", "fsdp", None), P("fsdp", "worker"), P("fsdp", "worker"))
    return jax.shard_map(shards, mesh=mesh, in_specs=in_specs, out_specs=out_specs, check_vma=False)
```

```python
import jax
import jax.numpy as jnp
from jax import lax
from jax.experimental import pallas as pl
from jax.experimental.pallas import tpu as pltpu
from jax.sharding import PartitionSpec as P

F32 = jnp.float32
BF16 = jnp.bfloat16
MESH = pl.DeviceIdType.MESH

TOK = 512
D = 4608
HALF = 512
R = 128
YB = 1152
XB = 288
ROWS = 72
WC = 4608
WH = 2304
SETS = 3


def ring(i):
    return lax.rem(i + 1, 4), lax.rem(i + 3, 4), lax.rem(i + 2, 4)


def step_of(top):
    q = top * (2.0**23 + 1.0)
    low = jnp.abs(q - q * (1.0 - 2.0**-24))
    return jnp.where(low < top, low * 0.5, low * 0.25)


def coded_of(delta, step):
    mag = jnp.abs(delta)
    level = jnp.where(mag >= 0.25 * step, 0.5, 0.0)
    level = jnp.where(mag >= 0.75 * step, 1.0, level)
    level = jnp.where(mag >= 1.25 * step, 1.5, level)
    level = jnp.where(mag >= 1.75 * step, 2.0, level)
    level = jnp.where(mag >= 2.5 * step, 3.0, level)
    level = jnp.where(mag >= 3.5 * step, 4.0, level)
    level = jnp.where(mag >= 5.0 * step, 6.0, level)
    coded = level * step
    return jnp.where(delta < 0, -coded, coded).astype(BF16)


def merge(a, b, bit, s):
    keep = jnp.where(bit, b, a)
    move = jnp.where(bit, pltpu.roll(b, s, 1), pltpu.roll(a, 128 - s, 1))
    return jnp.maximum(keep, move)


def code_chunk(delta_at, store):
    lane = lax.broadcasted_iota(jnp.int32, (ROWS, 128), 1)
    bit0, bit1, last = (lane & 1) == 1, (lane & 2) == 2, (lane & 28) == 28
    src = lax.broadcasted_iota(jnp.int32, (128, 512), 0)
    dst = lax.broadcasted_iota(jnp.int32, (128, 512), 1)
    spread = jnp.where(src == ((dst & 96) | 28 | (dst // 128)), 1.0, 0.0).astype(BF16)
    deltas, steps = [], []
    for k in range(SETS):
        four = [delta_at(4 * k + g) for g in range(4)]
        m = [jnp.abs(d) for d in four]
        top = merge(merge(m[0], m[1], bit0, 1), merge(m[2], m[3], bit0, 1), bit1, 2)
        for s in (4, 8, 16):
            top = jnp.maximum(top, pltpu.roll(top, s, 1))
        steps.append(jnp.where(last, step_of(top), 0.0))
        deltas.append(four)
    spread_steps = jnp.dot(
        jnp.concatenate(steps, axis=0).astype(BF16), spread, preferred_element_type=F32
    )
    for k in range(SETS):
        for g in range(4):
            step = spread_steps[ROWS * k:ROWS * (k + 1), 128 * g:128 * (g + 1)]
            store(4 * k + g, coded_of(deltas[k][g], step))


def kernel(
    x_in, w_in, g_in, loc_in, anc_in, mom_in,
    wg_out, na_out, nm_out,
    xs, gs, wraw, wa, wb, act, pa, pb,
    ra_o, ra_l, ra_r, rb_o, rb_l, rb_r,
    sa, sb, sa16, sb16,
    ta, tb,
    tt, fs_send, fs_recv, fz_send, fz_recv, wg_v,
    loc, anc, mom, cod, wo, wl, wr, na_v, nm_v,
    lsem, ssem, rsem,
):
    me = lax.axis_index("fsdp")
    wk = lax.axis_index("worker")
    c = lax.rem(me, 2)
    z = lax.rem(me // 2, 2)
    x = lax.rem(me // 4, 4)
    y = me // 16
    xr, xl, xo = ring(x)
    yr, yl, yo = ring(y)
    wr_i, wl_i, wo_i = ring(wk)
    hy, hx = YB // 2, XB // 2
    factor = D ** (-0.5)

    def dev(yy, xx, zz, cc):
        return (wk, ((yy * 4 + xx) * 2 + zz) * 2 + cc)

    sib = dev(y, x, z, 1 - c)
    zsame = dev(y, x, 1 - z, c)
    zother = dev(y, x, 1 - z, 1 - c)
    xright, xleft = dev(y, xr, z, c), dev(y, xl, z, c)
    yright, yleft = dev(yr, x, z, c), dev(yl, x, z, c)
    xopp, yopp = dev(y, xo, z, c), dev(yo, x, z, c)
    wright, wleft = (wr_i, me), (wl_i, me)

    pending = []

    def send(src, dst, to):
        k = len(pending)
        copy = pltpu.make_async_remote_copy(
            src_ref=src, dst_ref=dst, send_sem=ssem.at[k], recv_sem=rsem.at[k],
            device_id=to, device_id_type=MESH,
        )
        copy.start()
        pending.append(copy)
        return copy

    started = []

    def local(src, dst):
        copy = pltpu.make_async_copy(src, dst, lsem.at[len(started)])
        copy.start()
        started.append(copy)
        return copy

    def arrived(*copies):
        for copy in copies:
            copy.wait_recv()

    def cols(j):
        return pl.ds(pl.multiple_of(j * HALF, HALF), HALF)

    def wcols(j):
        return pl.ds(pl.multiple_of(j * WC, 128), WC)

    def half(ref, h):
        return ref.at[:, h * WH:(h + 1) * WH]

    def xrows(j):
        return pl.ds(pl.multiple_of(j * XB, 16), XB)

    def xrows_half(j, h):
        return pl.ds(pl.multiple_of(j * XB + h * hx, 16), hx)

    own_w = local(w_in.at[:, cols(c)], wraw.at[z, c])
    frag = {}
    for name, j in (("o", wo_i), ("r", wr_i), ("l", wl_i), ("s", wk)):
        frag[name] = (
            local(loc_in.at[:, wcols(j)], loc.at[j]),
            local(anc_in.at[:, wcols(j)], anc.at[j]),
        )
    own_x = local(x_in, xs.at[0])
    own_g = local(g_in.at[:, cols(c)], gs.at[0])
    own_m = local(mom_in, mom)

    barrier = pltpu.get_barrier_semaphore()
    partners = (sib, zsame, zother, xright, xleft, xopp, yright, yleft, yopp, wright, wleft)
    for p in partners:
        pl.semaphore_signal(barrier, inc=1, device_id=p, device_id_type=MESH)
    pl.semaphore_wait(barrier, len(partners))

    g1 = send(w_in.at[:, cols(c)], wraw.at[z, c], zsame)
    g2 = send(w_in.at[:, cols(1 - c)], wraw.at[z, c], zother)
    g0 = send(w_in.at[:, cols(1 - c)], wraw.at[z, c], sib)

    def code_block(name, j):
        for copy in frag[name]:
            copy.wait()

        def body(i, carry):
            def at(g):
                return pl.ds(pl.multiple_of((i * (4 * SETS) + g) * 128, 128), 128)

            def delta_at(g):
                return anc[j, :, at(g)].astype(F32) - loc[j, :, at(g)].astype(F32)

            def store(g, value):
                cod[j, :, at(g)] = value

            code_chunk(delta_at, store)
            return carry

        lax.fori_loop(0, WC // (512 * SETS), body, 0)

    state = [{}, {}]

    def gather1(s):
        mine_a, mine_b = wa.at[s, y, xrows(x)], wb.at[s, y, xrows(x)]
        out = []
        for a_to, b_to in ((xright, yright), (xleft, yleft), (xopp, yopp)):
            out.append(send(mine_a, mine_a, a_to))
            out.append(send(mine_b, mine_b, b_to))
        state[s]["g1"] = out

    def gather2(s):
        st = state[s]
        arrived(*st["g1"])
        a = (wa.at[s, y, 0:hy], wa.at[s, y, hy:YB])
        b = (wb.at[s, 0:2, xrows(x)], wb.at[s, 2:4, xrows(x)])
        st["g2"] = (
            send(a[0], a[0], yright), send(b[0], b[0], xright),
            send(a[1], a[1], yleft), send(b[1], b[1], xleft),
        )
        st["g3"] = [
            send(a[1], a[1], yright), send(b[1], b[1], xright),
            send(a[0], a[0], yleft), send(b[0], b[0], xleft),
        ]

    def gather2_next(s):
        st = state[s]
        steps = (
            (wa.at[s, yl, 0:hy], yright), (wb.at[s, 0:2, xrows(xl)], xright),
            (wa.at[s, yr, hy:YB], yleft), (wb.at[s, 2:4, xrows(xr)], xleft),
        )
        for copy, (ref, to) in zip(st["g2"], steps):
            arrived(copy)
            st["g3"].append(send(ref, ref, to))

    def forward(s):
        arrived(*state[s]["g3"])

        def body(i, carry):
            t = i // 2
            r = pl.ds(pl.multiple_of(lax.rem(i, 2) * 256, 256), 256)
            weight = jnp.concatenate([wa[s].reshape(D, R), wb[s].reshape(D, R)], axis=1)
            value = jnp.dot(xs[t, r, :], weight, preferred_element_type=F32) * factor
            sig = jax.nn.sigmoid(value)
            cot = gs[t, r, 2 * R * s:2 * R * (s + 1)].astype(F32)
            act[s, t, r, :] = (cot * sig * (1.0 + value * (1.0 - sig))).astype(BF16)
            return carry

        lax.fori_loop(0, 4, body, 0)

    def backward(s, yy):
        at = pl.ds(pl.multiple_of(yy * YB, 128), YB)
        dims = (((0,), (0,)), ((), ()))
        part = lax.dot_general(xs[0, :, at], act[s, 0], dims, preferred_element_type=F32)
        part += lax.dot_general(xs[1, :, at], act[s, 1], dims, preferred_element_type=F32)
        pa[s, yy] = part[:, :R].astype(BF16)
        pb[s, yy] = part[:, R:].astype(BF16)

    def reduce1(s):
        st = state[s]
        backward(s, yo)
        a0 = send(pa.at[s, yo, 0:hy], ra_o.at[s, 0], yright)
        a1 = send(pa.at[s, yo, hy:YB], ra_o.at[s, 1], yleft)
        backward(s, yr)
        a2 = send(pa.at[s, yr, hy:YB], ra_l.at[s, hy:YB], yright)
        backward(s, yl)
        a3 = send(pa.at[s, yl, 0:hy], ra_r.at[s, 0:hy], yleft)
        backward(s, y)
        b0 = send(pb.at[s, 0:2, xrows(xo)], rb_o.at[s, 0], xright)
        b1 = send(pb.at[s, 2:4, xrows(xo)], rb_o.at[s, 1], xleft)
        b2 = send(pb.at[s, 2:4, xrows(xr)], rb_l.at[s, 2:4], xright)
        b3 = send(pb.at[s, 0:2, xrows(xl)], rb_r.at[s, 0:2], xleft)
        st["r1"] = (a0, a1, b0, b1)
        st["ra"], st["rb"] = [a2, a3], [b2, b3]

    def add_to(dst, at, other, n):
        def body(i, carry):
            r = pl.ds(pl.multiple_of(i * 96, 16), 96)
            d = pl.ds(pl.multiple_of(at + i * 96, 16), 96)
            dst[d, :] = (dst[d, :].astype(F32) + other[r, :].astype(F32)).astype(BF16)
            return carry

        lax.fori_loop(0, n // 96, body, 0)

    def reduce1_next(s):
        st = state[s]
        a0, a1, b0, b1 = st["r1"]
        arrived(a0)
        add_to(pa.at[s, yr], 0, ra_o.at[s, 0], hy)
        st["ra"].append(send(pa.at[s, yr, 0:hy], ra_l.at[s, 0:hy], yright))
        arrived(a1)
        add_to(pa.at[s, yl], hy, ra_o.at[s, 1], hy)
        st["ra"].append(send(pa.at[s, yl, hy:YB], ra_r.at[s, hy:YB], yleft))
        arrived(b0)
        for k in range(2):
            add_to(pb.at[s, k], xr * XB, rb_o.at[s, 0, k], XB)
        st["rb"].append(send(pb.at[s, 0:2, xrows(xr)], rb_l.at[s, 0:2], xright))
        arrived(b1)
        for k in range(2):
            add_to(pb.at[s, 2 + k], xl * XB, rb_o.at[s, 1, k], XB)
        st["rb"].append(send(pb.at[s, 2:4, xrows(xl)], rb_r.at[s, 2:4], xleft))

    def reduce2(s):
        st = state[s]
        arrived(*st["ra"])

        def sum_a(i, carry):
            r = pl.ds(pl.multiple_of(i * 192, 96), 192)
            total = pa[s, y, r, :].astype(F32) + ra_l[s, r, :].astype(F32) + ra_r[s, r, :].astype(F32)
            sa[s, r, :] = total
            sa16[s, r, :] = total.astype(BF16)
            return carry

        lax.fori_loop(0, YB // 192, sum_a, 0)
        st["ta"] = [
            send(sa16.at[s, xrows(j)], ta.at[s, k], to)
            for k, (j, to) in enumerate(((xo, xopp), (xr, xright), (xl, xleft)))
        ]
        arrived(*st["rb"])

        def sum_b(k, carry):
            total = pb[s, k, xrows(x), :].astype(F32) + rb_l[s, k].astype(F32) + rb_r[s, k].astype(F32)
            sb[s, k] = total
            sb16[s, k] = total.astype(BF16)
            return carry

        lax.fori_loop(0, 4, sum_b, 0)
        st["tb"] = [
            send(sb16.at[s, j], tb.at[s, k], to)
            for k, (j, to) in enumerate(((yo, yopp), (yr, yright), (yl, yleft)))
        ]

    def part(zz, cc):
        return pl.ds(pl.multiple_of((zz * 2 + cc) * ROWS, 8), ROWS)

    def reduce3(s):
        st = state[s]
        arrived(*st["ta"])
        tt[s, :, 0:R] = sa[s, xrows(x), :] + (
            ta[s, 0].astype(F32) + ta[s, 1].astype(F32) + ta[s, 2].astype(F32)
        )
        arrived(*st["tb"])
        tt[s, :, R:2 * R] = sb[s, y] + (
            tb[s, 0].astype(F32) + tb[s, 1].astype(F32) + tb[s, 2].astype(F32)
        )
        for k in range(2):
            fz_send[s, k] = tt[s, part(1 - z, k), :].astype(BF16)
        f1 = send(fz_send.at[s, c], fz_recv.at[s, c], zsame)
        f2 = send(fz_send.at[s, 1 - c], fz_recv.at[s, c], zother)
        fs_send[s] = tt[s, part(z, 1 - c), :]
        f0 = send(fs_send.at[s], fs_recv.at[s], sib)
        st["f"] = (f1, f2, f0)

    def last(s):
        arrived(*state[s]["f"])

        def at(j):
            return pl.ds(pl.multiple_of(j * HALF + 2 * R * s, 2 * R), 2 * R)

        wg_v[:, at(c)] = (tt[s, part(z, c), :] + fz_recv[s, c].astype(F32)) * factor
        wg_v[:, at(1 - c)] = (fs_recv[s] + fz_recv[s, 1 - c].astype(F32)) * factor

    code_block("o", wo_i)
    w0 = send(half(cod.at[wo_i], 0), wo.at[0], wright)
    w1 = send(half(cod.at[wo_i], 1), wo.at[1], wleft)

    own_w.wait()
    arrived(g1, g2, g0)
    for zz in range(2):
        rows = jnp.concatenate(
            [wraw[zz, 0].astype(F32), wraw[zz, 1].astype(F32)], axis=0
        ).astype(BF16)
        for s in range(2):
            wa[s, y, xrows_half(x, zz), :] = rows[:, 2 * R * s:2 * R * s + R]
            wb[s, y, xrows_half(x, zz), :] = rows[:, 2 * R * s + R:2 * R * (s + 1)]

    gather1(0)
    gather1(1)
    sx = send(x_in, xs.at[1], sib)
    sg = send(g_in.at[:, cols(1 - c)], gs.at[1], sib)

    code_block("r", wr_i)
    w2 = send(half(cod.at[wr_i], 1), half(wl, 1), wright)
    gather2(0)
    code_block("l", wl_i)
    w3 = send(half(cod.at[wl_i], 0), half(wr, 0), wleft)
    gather2_next(0)
    gather2(1)
    code_block("s", wk)
    gather2_next(1)

    own_x.wait()
    own_g.wait()
    arrived(sx, sg)
    forward(0)

    arrived(w0, w1)
    for j, h in ((wr_i, 0), (wl_i, 1)):
        def body(i, carry, j=j, h=h):
            at = pl.ds(pl.multiple_of(i * 256, 256), 256)
            to = pl.ds(pl.multiple_of(h * WH + i * 256, 256), 256)
            cod[j, :, to] = (cod[j, :, to].astype(F32) + wo[h, :, at].astype(F32)).astype(BF16)
            return carry
        lax.fori_loop(0, WH // 256, body, 0)
    w4 = send(half(cod.at[wr_i], 0), half(wl, 0), wright)
    w5 = send(half(cod.at[wl_i], 1), half(wr, 1), wleft)

    reduce1(0)
    forward(1)
    reduce1_next(0)
    reduce1(1)
    reduce2(0)
    reduce1_next(1)

    arrived(w2, w3, w4, w5)
    own_m.wait()

    def outer(i, carry):
        at = pl.ds(pl.multiple_of(i * 256, 256), 256)
        total = cod[wk, :, at].astype(F32) + wl[:, at].astype(F32) + wr[:, at].astype(F32)
        grad = total * 0.25
        fresh = 0.9 * mom[:, at] + grad
        nm_v[:, at] = fresh
        na_v[:, at] = (anc[wk, :, at].astype(F32) - 0.7 * (grad + 0.9 * fresh)).astype(BF16)
        return carry

    lax.fori_loop(0, WC // 256, outer, 0)
    out1 = local(na_v, na_out)
    out2 = local(nm_v, nm_out)

    reduce3(0)
    reduce2(1)
    reduce3(1)
    last(0)
    last(1)
    out0 = local(wg_v, wg_out)
    for copy in pending:
        copy.wait_send()
    for copy in (out0, out1, out2):
        copy.wait()


def hand_on(wg_in, na_in, nm_in, wg_out, na_out, nm_out, sem):
    copies = [
        pltpu.make_async_copy(src, dst, sem.at[k])
        for k, (src, dst) in enumerate(((nm_in, nm_out), (na_in, na_out), (wg_in, wg_out)))
    ]
    for copy in copies:
        copy.start()
    for copy in copies:
        copy.wait()


def shards(inner_input, inner_weight, grad_out, local_fragment, anchor, momentum):
    any_spec = pl.BlockSpec(memory_space=pl.ANY)
    vm = pltpu.VMEM
    hy, hx = YB // 2, XB // 2
    wg, na, nm = pl.pallas_call(
        kernel,
        out_shape=(
            jax.ShapeDtypeStruct((ROWS, 1024), F32),
            jax.ShapeDtypeStruct((ROWS, WC), BF16),
            jax.ShapeDtypeStruct((ROWS, WC), F32),
        ),
        in_specs=[any_spec] * 6,
        out_specs=(any_spec,) * 3,
        scratch_shapes=[
            vm((2, TOK, D), BF16), vm((2, TOK, HALF), BF16), vm((2, 2, ROWS, HALF), BF16),
            vm((2, 4, YB, R), BF16), vm((2, 4, YB, R), BF16),
            vm((2, 2, TOK, 2 * R), BF16),
            vm((2, 4, YB, R), BF16), vm((2, 4, YB, R), BF16),
            vm((2, 2, hy, R), BF16), vm((2, YB, R), BF16), vm((2, YB, R), BF16),
            vm((2, 2, 2, XB, R), BF16), vm((2, 4, XB, R), BF16), vm((2, 4, XB, R), BF16),
            vm((2, YB, R), F32), vm((2, 4, XB, R), F32), vm((2, YB, R), BF16), vm((2, 4, XB, R), BF16),
            vm((2, 3, XB, R), BF16), vm((2, 3, XB, R), BF16),
            vm((2, XB, 2 * R), F32),
            vm((2, ROWS, 2 * R), F32), vm((2, ROWS, 2 * R), F32),
            vm((2, 2, ROWS, 2 * R), BF16), vm((2, 2, ROWS, 2 * R), BF16),
            vm((ROWS, 1024), F32),
            vm((4, ROWS, WC), BF16), vm((4, ROWS, WC), BF16), vm((ROWS, WC), F32),
            vm((4, ROWS, WC), BF16),
            vm((2, ROWS, WH), BF16), vm((ROWS, WC), BF16), vm((ROWS, WC), BF16),
            vm((ROWS, WC), BF16), vm((ROWS, WC), F32),
            pltpu.SemaphoreType.DMA((16,)),
            pltpu.SemaphoreType.DMA((100,)),
            pltpu.SemaphoreType.DMA((100,)),
        ],
        compiler_params=pltpu.CompilerParams(
            collective_id=0, has_side_effects=True, vmem_limit_bytes=60 * 1024 * 1024
        ),
        cost_estimate=pl.CostEstimate(
            flops=4 * TOK * D * 1024, bytes_accessed=16 * 1024 * 1024, transcendentals=TOK * 1024
        ),
    )(inner_input[0], inner_weight[0], grad_out[0], local_fragment[0], anchor, momentum)
    wg, na, nm = pl.pallas_call(
        hand_on,
        out_shape=tuple(jax.ShapeDtypeStruct(a.shape, a.dtype) for a in (wg, na, nm)),
        in_specs=[any_spec] * 3,
        out_specs=(any_spec,) * 3,
        scratch_shapes=[pltpu.SemaphoreType.DMA((3,))],
    )(wg, na, nm)
    return (wg[None], na, nm)


def solution(mesh):
    in_specs = (
        P("worker", "fsdp", None),
        P("worker", "fsdp", None),
        P("worker", "fsdp", None),
        P("worker", "fsdp", None),
        P("fsdp", None),
        P("fsdp", "worker"),
    )
    out_specs = (P("worker", "fsdp", None), P("fsdp", "worker"), P("fsdp", "worker"))
    return jax.shard_map(shards, mesh=mesh, in_specs=in_specs, out_specs=out_specs, check_vma=False)
```

```python
import jax
import jax.numpy as jnp
from jax import lax
from jax.experimental import pallas as pl
from jax.experimental.pallas import tpu as pltpu
from jax.sharding import PartitionSpec as P

F32 = jnp.float32
BF16 = jnp.bfloat16
MESH = pl.DeviceIdType.MESH

TOK = 512
D = 4608
HALF = 512
R = 128
YB = 1152
XB = 288
ROWS = 72
WC = 4608
WH = 2304
SETS = 3


def ring(i):
    return lax.rem(i + 1, 4), lax.rem(i + 3, 4), lax.rem(i + 2, 4)


def step_of(top):
    q = top * (2.0**23 + 1.0)
    low = jnp.abs(q - q * (1.0 - 2.0**-24))
    return jnp.where(low < top, low * 0.5, low * 0.25)


def coded_of(delta, step):
    mag = jnp.abs(delta)
    level = jnp.where(mag >= 0.25 * step, 0.5, 0.0)
    level = jnp.where(mag >= 0.75 * step, 1.0, level)
    level = jnp.where(mag >= 1.25 * step, 1.5, level)
    level = jnp.where(mag >= 1.75 * step, 2.0, level)
    level = jnp.where(mag >= 2.5 * step, 3.0, level)
    level = jnp.where(mag >= 3.5 * step, 4.0, level)
    level = jnp.where(mag >= 5.0 * step, 6.0, level)
    coded = level * step
    return jnp.where(delta < 0, -coded, coded).astype(BF16)


def merge(a, b, bit, s):
    keep = jnp.where(bit, b, a)
    move = jnp.where(bit, pltpu.roll(b, s, 1), pltpu.roll(a, 128 - s, 1))
    return jnp.maximum(keep, move)


def code_chunk(delta_at, store):
    lane = lax.broadcasted_iota(jnp.int32, (ROWS, 128), 1)
    bit0, bit1, last = (lane & 1) == 1, (lane & 2) == 2, (lane & 28) == 28
    src = lax.broadcasted_iota(jnp.int32, (128, 512), 0)
    dst = lax.broadcasted_iota(jnp.int32, (128, 512), 1)
    spread = jnp.where(src == ((dst & 96) | 28 | (dst // 128)), 1.0, 0.0).astype(BF16)
    deltas, steps = [], []
    for k in range(SETS):
        four = [delta_at(4 * k + g) for g in range(4)]
        m = [jnp.abs(d) for d in four]
        top = merge(merge(m[0], m[1], bit0, 1), merge(m[2], m[3], bit0, 1), bit1, 2)
        for s in (4, 8, 16):
            top = jnp.maximum(top, pltpu.roll(top, s, 1))
        steps.append(jnp.where(last, step_of(top), 0.0))
        deltas.append(four)
    spread_steps = jnp.dot(
        jnp.concatenate(steps, axis=0).astype(BF16), spread, preferred_element_type=F32
    )
    for k in range(SETS):
        for g in range(4):
            step = spread_steps[ROWS * k:ROWS * (k + 1), 128 * g:128 * (g + 1)]
            store(4 * k + g, coded_of(deltas[k][g], step))


def kernel(
    x_in, w_in, g_in, loc_in, anc_in, mom_in,
    wg_out, na_out, nm_out,
    xs, gs, wraw, wa, wb, act, pa, pb,
    ra_o, ra_l, ra_r, rb_o, rb_l, rb_r,
    sa, sb, sa16, sb16,
    ta, tb,
    tt, fs_send, fs_recv, fz_send, fz_recv, wg_v,
    loc, anc, mom, cod, wo, wl, wr, na_v, nm_v,
    lsem, ssem, rsem,
):
    me = lax.axis_index("fsdp")
    wk = lax.axis_index("worker")
    c = lax.rem(me, 2)
    z = lax.rem(me // 2, 2)
    x = lax.rem(me // 4, 4)
    y = me // 16
    xr, xl, xo = ring(x)
    yr, yl, yo = ring(y)
    wr_i, wl_i, wo_i = ring(wk)
    hy, hx = YB // 2, XB // 2
    factor = D ** (-0.5)

    def dev(yy, xx, zz, cc):
        return (wk, ((yy * 4 + xx) * 2 + zz) * 2 + cc)

    sib = dev(y, x, z, 1 - c)
    zsame = dev(y, x, 1 - z, c)
    zother = dev(y, x, 1 - z, 1 - c)
    xright, xleft = dev(y, xr, z, c), dev(y, xl, z, c)
    yright, yleft = dev(yr, x, z, c), dev(yl, x, z, c)
    xopp, yopp = dev(y, xo, z, c), dev(yo, x, z, c)
    wright, wleft = (wr_i, me), (wl_i, me)

    pending = []

    def send(src, dst, to):
        k = len(pending)
        copy = pltpu.make_async_remote_copy(
            src_ref=src, dst_ref=dst, send_sem=ssem.at[k], recv_sem=rsem.at[k],
            device_id=to, device_id_type=MESH,
        )
        copy.start()
        pending.append(copy)
        return copy

    started = []

    def local(src, dst):
        copy = pltpu.make_async_copy(src, dst, lsem.at[len(started)])
        copy.start()
        started.append(copy)
        return copy

    def arrived(*copies):
        for copy in copies:
            copy.wait_recv()

    def cols(j):
        return pl.ds(pl.multiple_of(j * HALF, HALF), HALF)

    def wcols(j):
        return pl.ds(pl.multiple_of(j * WC, 128), WC)

    def half(ref, h):
        return ref.at[:, h * WH:(h + 1) * WH]

    def xrows(j):
        return pl.ds(pl.multiple_of(j * XB, 16), XB)

    def xrows_half(j, h):
        return pl.ds(pl.multiple_of(j * XB + h * hx, 16), hx)

    own_w = local(w_in.at[:, cols(c)], wraw.at[z, c])
    frag = {}
    for name, j in (("o", wo_i), ("r", wr_i), ("l", wl_i), ("s", wk)):
        frag[name] = (
            local(loc_in.at[:, wcols(j)], loc.at[j]),
            local(anc_in.at[:, wcols(j)], anc.at[j]),
        )
    own_x = local(x_in, xs.at[0])
    own_g = local(g_in.at[:, cols(c)], gs.at[0])
    own_m = local(mom_in, mom)

    barrier = pltpu.get_barrier_semaphore()
    partners = (sib, zsame, zother, xright, xleft, xopp, yright, yleft, yopp, wright, wleft)
    for p in partners:
        pl.semaphore_signal(barrier, inc=1, device_id=p, device_id_type=MESH)
    pl.semaphore_wait(barrier, len(partners))

    g1 = send(w_in.at[:, cols(c)], wraw.at[z, c], zsame)
    g2 = send(w_in.at[:, cols(1 - c)], wraw.at[z, c], zother)
    g0 = send(w_in.at[:, cols(1 - c)], wraw.at[z, c], sib)

    def code_block(name, j):
        for copy in frag[name]:
            copy.wait()

        def body(i, carry):
            def at(g):
                return pl.ds(pl.multiple_of((i * (4 * SETS) + g) * 128, 128), 128)

            def delta_at(g):
                return anc[j, :, at(g)].astype(F32) - loc[j, :, at(g)].astype(F32)

            def store(g, value):
                cod[j, :, at(g)] = value

            code_chunk(delta_at, store)
            return carry

        lax.fori_loop(0, WC // (512 * SETS), body, 0)

    state = [{}, {}]

    def gather1(s):
        mine_a, mine_b = wa.at[s, y, xrows(x)], wb.at[s, y, xrows(x)]
        out = []
        for a_to, b_to in ((xright, yright), (xleft, yleft), (xopp, yopp)):
            out.append(send(mine_a, mine_a, a_to))
            out.append(send(mine_b, mine_b, b_to))
        state[s]["g1"] = out

    def gather2(s):
        st = state[s]
        arrived(*st["g1"])
        a = (wa.at[s, y, 0:hy], wa.at[s, y, hy:YB])
        b = (wb.at[s, 0:2, xrows(x)], wb.at[s, 2:4, xrows(x)])
        st["g2"] = (
            send(a[0], a[0], yright), send(b[0], b[0], xright),
            send(a[1], a[1], yleft), send(b[1], b[1], xleft),
        )
        st["g3"] = [
            send(a[1], a[1], yright), send(b[1], b[1], xright),
            send(a[0], a[0], yleft), send(b[0], b[0], xleft),
        ]

    def gather2_next(s):
        st = state[s]
        steps = (
            (wa.at[s, yl, 0:hy], yright), (wb.at[s, 0:2, xrows(xl)], xright),
            (wa.at[s, yr, hy:YB], yleft), (wb.at[s, 2:4, xrows(xr)], xleft),
        )
        for copy, (ref, to) in zip(st["g2"], steps):
            arrived(copy)
            st["g3"].append(send(ref, ref, to))

    def forward(s):
        arrived(*state[s]["g3"])

        def body(i, carry):
            t = i // 2
            r = pl.ds(pl.multiple_of(lax.rem(i, 2) * 256, 256), 256)
            weight = jnp.concatenate([wa[s].reshape(D, R), wb[s].reshape(D, R)], axis=1)
            value = jnp.dot(xs[t, r, :], weight, preferred_element_type=F32) * factor
            sig = jax.nn.sigmoid(value)
            cot = gs[t, r, 2 * R * s:2 * R * (s + 1)].astype(F32)
            act[s, t, r, :] = (cot * sig * (1.0 + value * (1.0 - sig))).astype(BF16)
            return carry

        lax.fori_loop(0, 4, body, 0)

    def backward(s, yy):
        at = pl.ds(pl.multiple_of(yy * YB, 128), YB)
        dims = (((0,), (0,)), ((), ()))
        part = lax.dot_general(xs[0, :, at], act[s, 0], dims, preferred_element_type=F32)
        part += lax.dot_general(xs[1, :, at], act[s, 1], dims, preferred_element_type=F32)
        pa[s, yy] = part[:, :R].astype(BF16)
        pb[s, yy] = part[:, R:].astype(BF16)

    def reduce1(s):
        st = state[s]
        backward(s, yo)
        a0 = send(pa.at[s, yo, 0:hy], ra_o.at[s, 0], yright)
        a1 = send(pa.at[s, yo, hy:YB], ra_o.at[s, 1], yleft)
        backward(s, yr)
        a2 = send(pa.at[s, yr, hy:YB], ra_l.at[s, hy:YB], yright)
        backward(s, yl)
        a3 = send(pa.at[s, yl, 0:hy], ra_r.at[s, 0:hy], yleft)
        backward(s, y)
        b0 = send(pb.at[s, 0:2, xrows(xo)], rb_o.at[s, 0], xright)
        b1 = send(pb.at[s, 2:4, xrows(xo)], rb_o.at[s, 1], xleft)
        b2 = send(pb.at[s, 2:4, xrows(xr)], rb_l.at[s, 2:4], xright)
        b3 = send(pb.at[s, 0:2, xrows(xl)], rb_r.at[s, 0:2], xleft)
        st["r1"] = (a0, a1, b0, b1)
        st["ra"], st["rb"] = [a2, a3], [b2, b3]

    def add_to(dst, at, other, n):
        def body(i, carry):
            r = pl.ds(pl.multiple_of(i * 96, 16), 96)
            d = pl.ds(pl.multiple_of(at + i * 96, 16), 96)
            dst[d, :] = (dst[d, :].astype(F32) + other[r, :].astype(F32)).astype(BF16)
            return carry

        lax.fori_loop(0, n // 96, body, 0)

    def reduce1_next(s):
        st = state[s]
        a0, a1, b0, b1 = st["r1"]
        arrived(a0)
        add_to(pa.at[s, yr], 0, ra_o.at[s, 0], hy)
        st["ra"].append(send(pa.at[s, yr, 0:hy], ra_l.at[s, 0:hy], yright))
        arrived(a1)
        add_to(pa.at[s, yl], hy, ra_o.at[s, 1], hy)
        st["ra"].append(send(pa.at[s, yl, hy:YB], ra_r.at[s, hy:YB], yleft))
        arrived(b0)
        for k in range(2):
            add_to(pb.at[s, k], xr * XB, rb_o.at[s, 0, k], XB)
        st["rb"].append(send(pb.at[s, 0:2, xrows(xr)], rb_l.at[s, 0:2], xright))
        arrived(b1)
        for k in range(2):
            add_to(pb.at[s, 2 + k], xl * XB, rb_o.at[s, 1, k], XB)
        st["rb"].append(send(pb.at[s, 2:4, xrows(xl)], rb_r.at[s, 2:4], xleft))

    def reduce2(s):
        st = state[s]
        arrived(*st["ra"])

        def sum_a(i, carry):
            r = pl.ds(pl.multiple_of(i * 192, 96), 192)
            total = pa[s, y, r, :].astype(F32) + ra_l[s, r, :].astype(F32) + ra_r[s, r, :].astype(F32)
            sa[s, r, :] = total
            sa16[s, r, :] = total.astype(BF16)
            return carry

        lax.fori_loop(0, YB // 192, sum_a, 0)
        st["ta"] = [
            send(sa16.at[s, xrows(j)], ta.at[s, k], to)
            for k, (j, to) in enumerate(((xo, xopp), (xr, xright), (xl, xleft)))
        ]
        arrived(*st["rb"])

        def sum_b(k, carry):
            total = pb[s, k, xrows(x), :].astype(F32) + rb_l[s, k].astype(F32) + rb_r[s, k].astype(F32)
            sb[s, k] = total
            sb16[s, k] = total.astype(BF16)
            return carry

        lax.fori_loop(0, 4, sum_b, 0)
        st["tb"] = [
            send(sb16.at[s, j], tb.at[s, k], to)
            for k, (j, to) in enumerate(((yo, yopp), (yr, yright), (yl, yleft)))
        ]

    def part(zz, cc):
        return pl.ds(pl.multiple_of((zz * 2 + cc) * ROWS, 8), ROWS)

    def reduce3(s):
        st = state[s]
        arrived(*st["ta"])
        tt[s, :, 0:R] = sa[s, xrows(x), :] + (
            ta[s, 0].astype(F32) + ta[s, 1].astype(F32) + ta[s, 2].astype(F32)
        )
        arrived(*st["tb"])
        tt[s, :, R:2 * R] = sb[s, y] + (
            tb[s, 0].astype(F32) + tb[s, 1].astype(F32) + tb[s, 2].astype(F32)
        )
        for k in range(2):
            fz_send[s, k] = tt[s, part(1 - z, k), :].astype(BF16)
        f1 = send(fz_send.at[s, c], fz_recv.at[s, c], zsame)
        f2 = send(fz_send.at[s, 1 - c], fz_recv.at[s, c], zother)
        fs_send[s] = tt[s, part(z, 1 - c), :]
        f0 = send(fs_send.at[s], fs_recv.at[s], sib)
        st["f"] = (f1, f2, f0)

    def last(s):
        arrived(*state[s]["f"])

        def at(j):
            return pl.ds(pl.multiple_of(j * HALF + 2 * R * s, 2 * R), 2 * R)

        wg_v[:, at(c)] = (tt[s, part(z, c), :] + fz_recv[s, c].astype(F32)) * factor
        wg_v[:, at(1 - c)] = (fs_recv[s] + fz_recv[s, 1 - c].astype(F32)) * factor

    code_block("o", wo_i)
    w0 = send(half(cod.at[wo_i], 0), wo.at[0], wright)
    w1 = send(half(cod.at[wo_i], 1), wo.at[1], wleft)

    own_w.wait()
    arrived(g1, g2, g0)
    for zz in range(2):
        rows = jnp.concatenate(
            [wraw[zz, 0].astype(F32), wraw[zz, 1].astype(F32)], axis=0
        ).astype(BF16)
        for s in range(2):
            wa[s, y, xrows_half(x, zz), :] = rows[:, 2 * R * s:2 * R * s + R]
            wb[s, y, xrows_half(x, zz), :] = rows[:, 2 * R * s + R:2 * R * (s + 1)]

    gather1(0)
    gather1(1)
    sx = send(x_in, xs.at[1], sib)
    sg = send(g_in.at[:, cols(1 - c)], gs.at[1], sib)

    code_block("r", wr_i)
    w2 = send(half(cod.at[wr_i], 1), half(wl, 1), wright)
    gather2(0)
    code_block("l", wl_i)
    w3 = send(half(cod.at[wl_i], 0), half(wr, 0), wleft)
    gather2_next(0)
    gather2(1)
    code_block("s", wk)
    gather2_next(1)

    own_x.wait()
    own_g.wait()
    arrived(sx, sg)
    forward(0)

    arrived(w0, w1)
    for j, h in ((wr_i, 0), (wl_i, 1)):
        def body(i, carry, j=j, h=h):
            at = pl.ds(pl.multiple_of(i * 256, 256), 256)
            to = pl.ds(pl.multiple_of(h * WH + i * 256, 256), 256)
            cod[j, :, to] = (cod[j, :, to].astype(F32) + wo[h, :, at].astype(F32)).astype(BF16)
            return carry
        lax.fori_loop(0, WH // 256, body, 0)
    w4 = send(half(cod.at[wr_i], 0), half(wl, 0), wright)
    w5 = send(half(cod.at[wl_i], 1), half(wr, 1), wleft)

    reduce1(0)
    forward(1)
    reduce1_next(0)
    reduce1(1)
    reduce2(0)
    reduce1_next(1)

    arrived(w2, w3, w4, w5)
    own_m.wait()

    def outer(i, carry):
        at = pl.ds(pl.multiple_of(i * 256, 256), 256)
        total = cod[wk, :, at].astype(F32) + wl[:, at].astype(F32) + wr[:, at].astype(F32)
        grad = total * 0.25
        fresh = 0.9 * mom[:, at] + grad
        nm_v[:, at] = fresh
        na_v[:, at] = (anc[wk, :, at].astype(F32) - 0.7 * (grad + 0.9 * fresh)).astype(BF16)
        return carry

    lax.fori_loop(0, WC // 256, outer, 0)
    out1 = local(na_v, na_out)
    out2 = local(nm_v, nm_out)

    reduce3(0)
    reduce2(1)
    reduce3(1)
    last(0)
    last(1)
    out0 = local(wg_v, wg_out)
    for copy in pending:
        copy.wait_send()
    for copy in (out0, out1, out2):
        copy.wait()


def hand_on(wg_in, na_in, nm_in, wg_out, na_out, nm_out, wg_v, na_v, nm_v, sem):
    arrays = ((nm_in, nm_v, nm_out), (na_in, na_v, na_out), (wg_in, wg_v, wg_out))
    reads = [pltpu.make_async_copy(a, v, sem.at[0, k]) for k, (a, v, b) in enumerate(arrays)]
    writes = [pltpu.make_async_copy(v, b, sem.at[1, k]) for k, (a, v, b) in enumerate(arrays)]
    for copy in reads:
        copy.start()
    for read, write in zip(reads, writes):
        read.wait()
        write.start()
    for copy in writes:
        copy.wait()


def shards(inner_input, inner_weight, grad_out, local_fragment, anchor, momentum):
    any_spec = pl.BlockSpec(memory_space=pl.ANY)
    vm = pltpu.VMEM
    hy, hx = YB // 2, XB // 2
    wg, na, nm = pl.pallas_call(
        kernel,
        out_shape=(
            jax.ShapeDtypeStruct((ROWS, 1024), F32),
            jax.ShapeDtypeStruct((ROWS, WC), BF16),
            jax.ShapeDtypeStruct((ROWS, WC), F32),
        ),
        in_specs=[any_spec] * 6,
        out_specs=(any_spec,) * 3,
        scratch_shapes=[
            vm((2, TOK, D), BF16), vm((2, TOK, HALF), BF16), vm((2, 2, ROWS, HALF), BF16),
            vm((2, 4, YB, R), BF16), vm((2, 4, YB, R), BF16),
            vm((2, 2, TOK, 2 * R), BF16),
            vm((2, 4, YB, R), BF16), vm((2, 4, YB, R), BF16),
            vm((2, 2, hy, R), BF16), vm((2, YB, R), BF16), vm((2, YB, R), BF16),
            vm((2, 2, 2, XB, R), BF16), vm((2, 4, XB, R), BF16), vm((2, 4, XB, R), BF16),
            vm((2, YB, R), F32), vm((2, 4, XB, R), F32), vm((2, YB, R), BF16), vm((2, 4, XB, R), BF16),
            vm((2, 3, XB, R), BF16), vm((2, 3, XB, R), BF16),
            vm((2, XB, 2 * R), F32),
            vm((2, ROWS, 2 * R), F32), vm((2, ROWS, 2 * R), F32),
            vm((2, 2, ROWS, 2 * R), BF16), vm((2, 2, ROWS, 2 * R), BF16),
            vm((ROWS, 1024), F32),
            vm((4, ROWS, WC), BF16), vm((4, ROWS, WC), BF16), vm((ROWS, WC), F32),
            vm((4, ROWS, WC), BF16),
            vm((2, ROWS, WH), BF16), vm((ROWS, WC), BF16), vm((ROWS, WC), BF16),
            vm((ROWS, WC), BF16), vm((ROWS, WC), F32),
            pltpu.SemaphoreType.DMA((16,)),
            pltpu.SemaphoreType.DMA((100,)),
            pltpu.SemaphoreType.DMA((100,)),
        ],
        compiler_params=pltpu.CompilerParams(
            collective_id=0, has_side_effects=True, vmem_limit_bytes=60 * 1024 * 1024
        ),
        cost_estimate=pl.CostEstimate(
            flops=4 * TOK * D * 1024, bytes_accessed=16 * 1024 * 1024, transcendentals=TOK * 1024
        ),
    )(inner_input[0], inner_weight[0], grad_out[0], local_fragment[0], anchor, momentum)
    wg, na, nm = pl.pallas_call(
        hand_on,
        out_shape=tuple(jax.ShapeDtypeStruct(a.shape, a.dtype) for a in (wg, na, nm)),
        in_specs=[any_spec] * 3,
        out_specs=(any_spec,) * 3,
        scratch_shapes=[vm(a.shape, a.dtype) for a in (wg, na, nm)] + [pltpu.SemaphoreType.DMA((2, 3))],
    )(wg, na, nm)
    return (wg[None], na, nm)


def solution(mesh):
    in_specs = (
        P("worker", "fsdp", None),
        P("worker", "fsdp", None),
        P("worker", "fsdp", None),
        P("worker", "fsdp", None),
        P("fsdp", None),
        P("fsdp", "worker"),
    )
    out_specs = (P("worker", "fsdp", None), P("fsdp", "worker"), P("fsdp", "worker"))
    return jax.shard_map(shards, mesh=mesh, in_specs=in_specs, out_specs=out_specs, check_vma=False)
```

```python
import jax
import jax.numpy as jnp
from jax import lax
from jax.experimental import pallas as pl
from jax.experimental.pallas import tpu as pltpu
from jax.sharding import PartitionSpec as P

F32 = jnp.float32
BF16 = jnp.bfloat16
MESH = pl.DeviceIdType.MESH

TOK = 512
D = 4608
HALF = 512
R = 128
YB = 1152
XB = 288
ROWS = 72
WC = 4608
WH = 2304
SETS = 3


def ring(i):
    return lax.rem(i + 1, 4), lax.rem(i + 3, 4), lax.rem(i + 2, 4)


def step_of(top):
    q = top * (2.0**23 + 1.0)
    low = jnp.abs(q - q * (1.0 - 2.0**-24))
    return jnp.where(low < top, low * 0.5, low * 0.25)


def coded_of(delta, step):
    mag = jnp.abs(delta)
    level = jnp.where(mag >= 0.25 * step, 0.5, 0.0)
    level = jnp.where(mag >= 0.75 * step, 1.0, level)
    level = jnp.where(mag >= 1.25 * step, 1.5, level)
    level = jnp.where(mag >= 1.75 * step, 2.0, level)
    level = jnp.where(mag >= 2.5 * step, 3.0, level)
    level = jnp.where(mag >= 3.5 * step, 4.0, level)
    level = jnp.where(mag >= 5.0 * step, 6.0, level)
    coded = level * step
    return jnp.where(delta < 0, -coded, coded).astype(BF16)


def merge(a, b, bit, s):
    keep = jnp.where(bit, b, a)
    move = jnp.where(bit, pltpu.roll(b, s, 1), pltpu.roll(a, 128 - s, 1))
    return jnp.maximum(keep, move)


def code_chunk(delta_at, store):
    lane = lax.broadcasted_iota(jnp.int32, (ROWS, 128), 1)
    bit0, bit1, last = (lane & 1) == 1, (lane & 2) == 2, (lane & 28) == 28
    src = lax.broadcasted_iota(jnp.int32, (128, 512), 0)
    dst = lax.broadcasted_iota(jnp.int32, (128, 512), 1)
    spread = jnp.where(src == ((dst & 96) | 28 | (dst // 128)), 1.0, 0.0).astype(BF16)
    deltas, steps = [], []
    for k in range(SETS):
        four = [delta_at(4 * k + g) for g in range(4)]
        m = [jnp.abs(d) for d in four]
        top = merge(merge(m[0], m[1], bit0, 1), merge(m[2], m[3], bit0, 1), bit1, 2)
        for s in (4, 8, 16):
            top = jnp.maximum(top, pltpu.roll(top, s, 1))
        steps.append(jnp.where(last, step_of(top), 0.0))
        deltas.append(four)
    spread_steps = jnp.dot(
        jnp.concatenate(steps, axis=0).astype(BF16), spread, preferred_element_type=F32
    )
    for k in range(SETS):
        for g in range(4):
            step = spread_steps[ROWS * k:ROWS * (k + 1), 128 * g:128 * (g + 1)]
            store(4 * k + g, coded_of(deltas[k][g], step))


def kernel(
    x_in, w_in, g_in, loc_in, anc_in, mom_in,
    wg_out, na_out, nm_out,
    xs, gs, wraw, wa, wb, act, pa, pb,
    ra_o, ra_l, ra_r, rb_o, rb_l, rb_r,
    sa, sb, sa16, sb16,
    ta, tb,
    tt, fs_send, fs_recv, fz_send, fz_recv, wg_v,
    loc, anc, mom, cod, wo, wl, wr, na_v, nm_v,
    lsem, ssem, rsem,
):
    me = lax.axis_index("fsdp")
    wk = lax.axis_index("worker")
    c = lax.rem(me, 2)
    z = lax.rem(me // 2, 2)
    x = lax.rem(me // 4, 4)
    y = me // 16
    xr, xl, xo = ring(x)
    yr, yl, yo = ring(y)
    wr_i, wl_i, wo_i = ring(wk)
    hy, hx = YB // 2, XB // 2
    factor = D ** (-0.5)

    def dev(yy, xx, zz, cc):
        return (wk, ((yy * 4 + xx) * 2 + zz) * 2 + cc)

    sib = dev(y, x, z, 1 - c)
    zsame = dev(y, x, 1 - z, c)
    zother = dev(y, x, 1 - z, 1 - c)
    xright, xleft = dev(y, xr, z, c), dev(y, xl, z, c)
    yright, yleft = dev(yr, x, z, c), dev(yl, x, z, c)
    xopp, yopp = dev(y, xo, z, c), dev(yo, x, z, c)
    wright, wleft = (wr_i, me), (wl_i, me)

    pending = []

    def send(src, dst, to):
        k = len(pending)
        copy = pltpu.make_async_remote_copy(
            src_ref=src, dst_ref=dst, send_sem=ssem.at[k], recv_sem=rsem.at[k],
            device_id=to, device_id_type=MESH,
        )
        copy.start()
        pending.append(copy)
        return copy

    started = []

    def local(src, dst):
        copy = pltpu.make_async_copy(src, dst, lsem.at[len(started)])
        copy.start()
        started.append(copy)
        return copy

    def arrived(*copies):
        for copy in copies:
            copy.wait_recv()

    def cols(j):
        return pl.ds(pl.multiple_of(j * HALF, HALF), HALF)

    def wcols(j):
        return pl.ds(pl.multiple_of(j * WC, 128), WC)

    def half(ref, h):
        return ref.at[:, h * WH:(h + 1) * WH]

    def xrows(j):
        return pl.ds(pl.multiple_of(j * XB, 16), XB)

    def xrows_half(j, h):
        return pl.ds(pl.multiple_of(j * XB + h * hx, 16), hx)

    own_w = local(w_in.at[:, cols(c)], wraw.at[z, c])
    frag = {}
    for name, j in (("o", wo_i), ("r", wr_i), ("l", wl_i), ("s", wk)):
        frag[name] = (
            local(loc_in.at[:, wcols(j)], loc.at[j]),
            local(anc_in.at[:, wcols(j)], anc.at[j]),
        )
    own_x = local(x_in, xs.at[0])
    own_g = local(g_in.at[:, cols(c)], gs.at[0])
    own_m = local(mom_in, mom)

    barrier = pltpu.get_barrier_semaphore()
    partners = (sib, zsame, zother, xright, xleft, xopp, yright, yleft, yopp, wright, wleft)
    for p in partners:
        pl.semaphore_signal(barrier, inc=1, device_id=p, device_id_type=MESH)
    pl.semaphore_wait(barrier, len(partners))

    g1 = send(w_in.at[:, cols(c)], wraw.at[z, c], zsame)
    g2 = send(w_in.at[:, cols(1 - c)], wraw.at[z, c], zother)
    g0 = send(w_in.at[:, cols(1 - c)], wraw.at[z, c], sib)

    def code_block(name, j):
        for copy in frag[name]:
            copy.wait()

        def body(i, carry):
            def at(g):
                return pl.ds(pl.multiple_of((i * (4 * SETS) + g) * 128, 128), 128)

            def delta_at(g):
                return anc[j, :, at(g)].astype(F32) - loc[j, :, at(g)].astype(F32)

            def store(g, value):
                cod[j, :, at(g)] = value

            code_chunk(delta_at, store)
            return carry

        lax.fori_loop(0, WC // (512 * SETS), body, 0)

    state = [{}, {}]

    def gather1(s):
        mine_a, mine_b = wa.at[s, y, xrows(x)], wb.at[s, y, xrows(x)]
        out = []
        for a_to, b_to in ((xright, yright), (xleft, yleft), (xopp, yopp)):
            out.append(send(mine_a, mine_a, a_to))
            out.append(send(mine_b, mine_b, b_to))
        state[s]["g1"] = out

    def gather2(s):
        st = state[s]
        arrived(*st["g1"])
        a = (wa.at[s, y, 0:hy], wa.at[s, y, hy:YB])
        b = (wb.at[s, 0:2, xrows(x)], wb.at[s, 2:4, xrows(x)])
        st["g2"] = (
            send(a[0], a[0], yright), send(b[0], b[0], xright),
            send(a[1], a[1], yleft), send(b[1], b[1], xleft),
        )
        st["g3"] = [
            send(a[1], a[1], yright), send(b[1], b[1], xright),
            send(a[0], a[0], yleft), send(b[0], b[0], xleft),
        ]

    def gather2_next(s):
        st = state[s]
        steps = (
            (wa.at[s, yl, 0:hy], yright), (wb.at[s, 0:2, xrows(xl)], xright),
            (wa.at[s, yr, hy:YB], yleft), (wb.at[s, 2:4, xrows(xr)], xleft),
        )
        for copy, (ref, to) in zip(st["g2"], steps):
            arrived(copy)
            st["g3"].append(send(ref, ref, to))

    def forward(s, t):
        if t == 0:
            arrived(*state[s]["g3"])

        def body(i, carry):
            r = pl.ds(pl.multiple_of(i * 256, 256), 256)
            weight = jnp.concatenate([wa[s].reshape(D, R), wb[s].reshape(D, R)], axis=1)
            value = jnp.dot(xs[t, r, :], weight, preferred_element_type=F32) * factor
            sig = jax.nn.sigmoid(value)
            cot = gs[t, r, 2 * R * s:2 * R * (s + 1)].astype(F32)
            act[s, t, r, :] = (cot * sig * (1.0 + value * (1.0 - sig))).astype(BF16)
            return carry

        lax.fori_loop(0, 2, body, 0)

    def backward(s, yy, slot):
        at = pl.ds(pl.multiple_of(yy * YB, 128), YB)
        dims = (((0,), (0,)), ((), ()))
        part = lax.dot_general(xs[0, :, at], act[s, 0], dims, preferred_element_type=F32)
        part += lax.dot_general(xs[1, :, at], act[s, 1], dims, preferred_element_type=F32)
        pa[s, yy] = part[:, :R].astype(BF16)
        pb[s, slot] = part[:, R:].astype(BF16)

    def reduce1(s):
        st = state[s]
        backward(s, yo, 0)
        a0 = send(pa.at[s, yo, 0:hy], ra_o.at[s, 0], yright)
        a1 = send(pa.at[s, yo, hy:YB], ra_o.at[s, 1], yleft)
        backward(s, yr, 1)
        b0 = send(pb.at[s, 0:2, xrows(xo)], rb_o.at[s, 0], xright)
        b3 = send(pb.at[s, 0:2, xrows(xl)], rb_r.at[s, 0:2], xleft)
        a2 = send(pa.at[s, yr, hy:YB], ra_l.at[s, hy:YB], yright)
        backward(s, yl, 2)
        a3 = send(pa.at[s, yl, 0:hy], ra_r.at[s, 0:hy], yleft)
        backward(s, y, 3)
        b1 = send(pb.at[s, 2:4, xrows(xo)], rb_o.at[s, 1], xleft)
        b2 = send(pb.at[s, 2:4, xrows(xr)], rb_l.at[s, 2:4], xright)
        st["r1"] = (a0, a1, b0, b1)
        st["ra"], st["rb"] = [a2, a3], [b2, b3]

    def add_to(dst, at, other, n):
        def body(i, carry):
            r = pl.ds(pl.multiple_of(i * 96, 16), 96)
            d = pl.ds(pl.multiple_of(at + i * 96, 16), 96)
            dst[d, :] = (dst[d, :].astype(F32) + other[r, :].astype(F32)).astype(BF16)
            return carry

        lax.fori_loop(0, n // 96, body, 0)

    def reduce1_next(s):
        st = state[s]
        a0, a1, b0, b1 = st["r1"]
        arrived(a0)
        add_to(pa.at[s, yr], 0, ra_o.at[s, 0], hy)
        st["ra"].append(send(pa.at[s, yr, 0:hy], ra_l.at[s, 0:hy], yright))
        arrived(a1)
        add_to(pa.at[s, yl], hy, ra_o.at[s, 1], hy)
        st["ra"].append(send(pa.at[s, yl, hy:YB], ra_r.at[s, hy:YB], yleft))
        arrived(b0)
        for k in range(2):
            add_to(pb.at[s, k], xr * XB, rb_o.at[s, 0, k], XB)
        st["rb"].append(send(pb.at[s, 0:2, xrows(xr)], rb_l.at[s, 0:2], xright))
        arrived(b1)
        for k in range(2):
            add_to(pb.at[s, 2 + k], xl * XB, rb_o.at[s, 1, k], XB)
        st["rb"].append(send(pb.at[s, 2:4, xrows(xl)], rb_r.at[s, 2:4], xleft))

    def reduce2(s):
        st = state[s]
        arrived(*st["ra"])

        def sum_a(i, carry):
            r = pl.ds(pl.multiple_of(i * 192, 96), 192)
            total = pa[s, y, r, :].astype(F32) + ra_l[s, r, :].astype(F32) + ra_r[s, r, :].astype(F32)
            sa[s, r, :] = total
            sa16[s, r, :] = total.astype(BF16)
            return carry

        lax.fori_loop(0, YB // 192, sum_a, 0)
        st["ta"] = [
            send(sa16.at[s, xrows(j)], ta.at[s, k], to)
            for k, (j, to) in enumerate(((xo, xopp), (xr, xright), (xl, xleft)))
        ]
        arrived(*st["rb"])

        def sum_b(k, carry):
            total = pb[s, k, xrows(x), :].astype(F32) + rb_l[s, k].astype(F32) + rb_r[s, k].astype(F32)
            sb[s, k] = total
            sb16[s, k] = total.astype(BF16)
            return carry

        lax.fori_loop(0, 4, sum_b, 0)
        st["tb"] = [
            send(sb16.at[s, k], tb.at[s, k], to) for k, to in enumerate((yopp, yright, yleft))
        ]

    def part(zz, cc):
        return pl.ds(pl.multiple_of((zz * 2 + cc) * ROWS, 8), ROWS)

    def reduce3(s):
        st = state[s]
        arrived(*st["ta"])
        tt[s, :, 0:R] = sa[s, xrows(x), :] + (
            ta[s, 0].astype(F32) + ta[s, 1].astype(F32) + ta[s, 2].astype(F32)
        )
        arrived(*st["tb"])
        tt[s, :, R:2 * R] = sb[s, 3] + (
            tb[s, 0].astype(F32) + tb[s, 1].astype(F32) + tb[s, 2].astype(F32)
        )
        for k in range(2):
            fz_send[s, k] = tt[s, part(1 - z, k), :].astype(BF16)
        f1 = send(fz_send.at[s, c], fz_recv.at[s, c], zsame)
        f2 = send(fz_send.at[s, 1 - c], fz_recv.at[s, c], zother)
        fs_send[s] = tt[s, part(z, 1 - c), :]
        f0 = send(fs_send.at[s], fs_recv.at[s], sib)
        st["f"] = (f1, f2, f0)

    def last(s):
        arrived(*state[s]["f"])

        def at(j):
            return pl.ds(pl.multiple_of(j * HALF + 2 * R * s, 2 * R), 2 * R)

        wg_v[:, at(c)] = (tt[s, part(z, c), :] + fz_recv[s, c].astype(F32)) * factor
        wg_v[:, at(1 - c)] = (fs_recv[s] + fz_recv[s, 1 - c].astype(F32)) * factor

    code_block("o", wo_i)

    own_w.wait()
    arrived(g1, g2, g0)
    for zz in range(2):
        rows = jnp.concatenate(
            [wraw[zz, 0].astype(F32), wraw[zz, 1].astype(F32)], axis=0
        ).astype(BF16)
        for s in range(2):
            wa[s, y, xrows_half(x, zz), :] = rows[:, 2 * R * s:2 * R * s + R]
            wb[s, y, xrows_half(x, zz), :] = rows[:, 2 * R * s + R:2 * R * (s + 1)]

    gather1(0)
    gather1(1)
    w0 = send(half(cod.at[wo_i], 0), wo.at[0], wright)
    w1 = send(half(cod.at[wo_i], 1), wo.at[1], wleft)
    sx = send(x_in, xs.at[1], sib)
    sg = send(g_in.at[:, cols(1 - c)], gs.at[1], sib)

    code_block("r", wr_i)
    w2 = send(half(cod.at[wr_i], 1), half(wl, 1), wright)
    gather2(0)
    code_block("l", wl_i)
    w3 = send(half(cod.at[wl_i], 0), half(wr, 0), wleft)
    gather2_next(0)
    gather2(1)
    code_block("s", wk)

    own_x.wait()
    own_g.wait()
    arrived(sx, sg)
    forward(0, 0)
    gather2_next(1)
    forward(0, 1)
    reduce1(0)

    arrived(w0, w1)
    for j, h in ((wr_i, 0), (wl_i, 1)):
        def body(i, carry, j=j, h=h):
            at = pl.ds(pl.multiple_of(i * 256, 256), 256)
            to = pl.ds(pl.multiple_of(h * WH + i * 256, 256), 256)
            cod[j, :, to] = (cod[j, :, to].astype(F32) + wo[h, :, at].astype(F32)).astype(BF16)
            return carry
        lax.fori_loop(0, WH // 256, body, 0)
    w4 = send(half(cod.at[wr_i], 0), half(wl, 0), wright)
    w5 = send(half(cod.at[wl_i], 1), half(wr, 1), wleft)

    forward(1, 0)
    forward(1, 1)
    reduce1_next(0)
    reduce1(1)
    reduce2(0)
    reduce1_next(1)

    arrived(w2, w3, w4, w5)
    own_m.wait()

    def outer(i, carry):
        at = pl.ds(pl.multiple_of(i * 256, 256), 256)
        total = cod[wk, :, at].astype(F32) + wl[:, at].astype(F32) + wr[:, at].astype(F32)
        grad = total * 0.25
        fresh = 0.9 * mom[:, at] + grad
        nm_v[:, at] = fresh
        na_v[:, at] = (anc[wk, :, at].astype(F32) - 0.7 * (grad + 0.9 * fresh)).astype(BF16)
        return carry

    lax.fori_loop(0, WC // 256, outer, 0)
    out1 = local(na_v, na_out)
    out2 = local(nm_v, nm_out)

    reduce3(0)
    reduce2(1)
    reduce3(1)
    last(0)
    last(1)
    out0 = local(wg_v, wg_out)
    for copy in pending:
        copy.wait_send()
    for copy in (out0, out1, out2):
        copy.wait()


def hand_on(wg_in, na_in, nm_in, wg_out, na_out, nm_out, wg_v, na_v, nm_v, sem):
    arrays = ((nm_in, nm_v, nm_out), (na_in, na_v, na_out), (wg_in, wg_v, wg_out))
    reads = [pltpu.make_async_copy(a, v, sem.at[0, k]) for k, (a, v, b) in enumerate(arrays)]
    writes = [pltpu.make_async_copy(v, b, sem.at[1, k]) for k, (a, v, b) in enumerate(arrays)]
    for copy in reads:
        copy.start()
    for read, write in zip(reads, writes):
        read.wait()
        write.start()
    for copy in writes:
        copy.wait()


def shards(inner_input, inner_weight, grad_out, local_fragment, anchor, momentum):
    any_spec = pl.BlockSpec(memory_space=pl.ANY)
    vm = pltpu.VMEM
    hy, hx = YB // 2, XB // 2
    wg, na, nm = pl.pallas_call(
        kernel,
        out_shape=(
            jax.ShapeDtypeStruct((ROWS, 1024), F32),
            jax.ShapeDtypeStruct((ROWS, WC), BF16),
            jax.ShapeDtypeStruct((ROWS, WC), F32),
        ),
        in_specs=[any_spec] * 6,
        out_specs=(any_spec,) * 3,
        scratch_shapes=[
            vm((2, TOK, D), BF16), vm((2, TOK, HALF), BF16), vm((2, 2, ROWS, HALF), BF16),
            vm((2, 4, YB, R), BF16), vm((2, 4, YB, R), BF16),
            vm((2, 2, TOK, 2 * R), BF16),
            vm((2, 4, YB, R), BF16), vm((2, 4, YB, R), BF16),
            vm((2, 2, hy, R), BF16), vm((2, YB, R), BF16), vm((2, YB, R), BF16),
            vm((2, 2, 2, XB, R), BF16), vm((2, 4, XB, R), BF16), vm((2, 4, XB, R), BF16),
            vm((2, YB, R), F32), vm((2, 4, XB, R), F32), vm((2, YB, R), BF16), vm((2, 4, XB, R), BF16),
            vm((2, 3, XB, R), BF16), vm((2, 3, XB, R), BF16),
            vm((2, XB, 2 * R), F32),
            vm((2, ROWS, 2 * R), F32), vm((2, ROWS, 2 * R), F32),
            vm((2, 2, ROWS, 2 * R), BF16), vm((2, 2, ROWS, 2 * R), BF16),
            vm((ROWS, 1024), F32),
            vm((4, ROWS, WC), BF16), vm((4, ROWS, WC), BF16), vm((ROWS, WC), F32),
            vm((4, ROWS, WC), BF16),
            vm((2, ROWS, WH), BF16), vm((ROWS, WC), BF16), vm((ROWS, WC), BF16),
            vm((ROWS, WC), BF16), vm((ROWS, WC), F32),
            pltpu.SemaphoreType.DMA((16,)),
            pltpu.SemaphoreType.DMA((100,)),
            pltpu.SemaphoreType.DMA((100,)),
        ],
        compiler_params=pltpu.CompilerParams(
            collective_id=0, has_side_effects=True, vmem_limit_bytes=60 * 1024 * 1024
        ),
        cost_estimate=pl.CostEstimate(
            flops=4 * TOK * D * 1024, bytes_accessed=16 * 1024 * 1024, transcendentals=TOK * 1024
        ),
    )(inner_input[0], inner_weight[0], grad_out[0], local_fragment[0], anchor, momentum)
    wg, na, nm = pl.pallas_call(
        hand_on,
        out_shape=tuple(jax.ShapeDtypeStruct(a.shape, a.dtype) for a in (wg, na, nm)),
        in_specs=[any_spec] * 3,
        out_specs=(any_spec,) * 3,
        scratch_shapes=[vm(a.shape, a.dtype) for a in (wg, na, nm)] + [pltpu.SemaphoreType.DMA((2, 3))],
    )(wg, na, nm)
    return (wg[None], na, nm)


def solution(mesh):
    in_specs = (
        P("worker", "fsdp", None),
        P("worker", "fsdp", None),
        P("worker", "fsdp", None),
        P("worker", "fsdp", None),
        P("fsdp", None),
        P("fsdp", "worker"),
    )
    out_specs = (P("worker", "fsdp", None), P("fsdp", "worker"), P("fsdp", "worker"))
    return jax.shard_map(shards, mesh=mesh, in_specs=in_specs, out_specs=out_specs, check_vma=False)
```

```python
import jax
import jax.numpy as jnp
from jax import lax
from jax.experimental import pallas as pl
from jax.experimental.pallas import tpu as pltpu
from jax.sharding import PartitionSpec as P

F32 = jnp.float32
BF16 = jnp.bfloat16
MESH = pl.DeviceIdType.MESH

TOK = 512
D = 4608
HALF = 512
R = 128
YB = 1152
XB = 288
ROWS = 72
WC = 4608
WH = 2304
SETS = 3


def ring(i):
    return lax.rem(i + 1, 4), lax.rem(i + 3, 4), lax.rem(i + 2, 4)


def step_of(top):
    q = top * (2.0**23 + 1.0)
    low = jnp.abs(q - q * (1.0 - 2.0**-24))
    return jnp.where(low < top, low * 0.5, low * 0.25)


def coded_of(delta, step):
    mag = jnp.abs(delta)
    level = jnp.where(mag >= 0.25 * step, 0.5, 0.0)
    level = jnp.where(mag >= 0.75 * step, 1.0, level)
    level = jnp.where(mag >= 1.25 * step, 1.5, level)
    level = jnp.where(mag >= 1.75 * step, 2.0, level)
    level = jnp.where(mag >= 2.5 * step, 3.0, level)
    level = jnp.where(mag >= 3.5 * step, 4.0, level)
    level = jnp.where(mag >= 5.0 * step, 6.0, level)
    coded = level * step
    return jnp.where(delta < 0, -coded, coded).astype(BF16)


def merge(a, b, bit, s):
    keep = jnp.where(bit, b, a)
    move = jnp.where(bit, pltpu.roll(b, s, 1), pltpu.roll(a, 128 - s, 1))
    return jnp.maximum(keep, move)


def code_chunk(delta_at, store):
    lane = lax.broadcasted_iota(jnp.int32, (ROWS, 128), 1)
    bit0, bit1, last = (lane & 1) == 1, (lane & 2) == 2, (lane & 28) == 28
    src = lax.broadcasted_iota(jnp.int32, (128, 512), 0)
    dst = lax.broadcasted_iota(jnp.int32, (128, 512), 1)
    spread = jnp.where(src == ((dst & 96) | 28 | (dst // 128)), 1.0, 0.0).astype(BF16)
    deltas, steps = [], []
    for k in range(SETS):
        four = [delta_at(4 * k + g) for g in range(4)]
        m = [jnp.abs(d) for d in four]
        top = merge(merge(m[0], m[1], bit0, 1), merge(m[2], m[3], bit0, 1), bit1, 2)
        for s in (4, 8, 16):
            top = jnp.maximum(top, pltpu.roll(top, s, 1))
        steps.append(jnp.where(last, step_of(top), 0.0))
        deltas.append(four)
    spread_steps = jnp.dot(
        jnp.concatenate(steps, axis=0).astype(BF16), spread, preferred_element_type=F32
    )
    for k in range(SETS):
        for g in range(4):
            step = spread_steps[ROWS * k:ROWS * (k + 1), 128 * g:128 * (g + 1)]
            store(4 * k + g, coded_of(deltas[k][g], step))


def kernel(
    x_in, w_in, g_in, loc_in, anc_in, mom_in,
    wg_out, na_out, nm_out,
    xs, gs, wraw, wa, wb, act, pa, pb,
    ra_o, ra_l, ra_r, rb_o, rb_l, rb_r,
    sa, sb, sa16, sb16,
    ta, tb,
    tt, fs_send, fs_recv, fz_send, fz_recv, wg_v,
    loc, anc, mom, cod, wo, wl, wr, na_v, nm_v,
    lsem, ssem, rsem,
):
    me = lax.axis_index("fsdp")
    wk = lax.axis_index("worker")
    c = lax.rem(me, 2)
    z = lax.rem(me // 2, 2)
    x = lax.rem(me // 4, 4)
    y = me // 16
    xr, xl, xo = ring(x)
    yr, yl, yo = ring(y)
    wr_i, wl_i, wo_i = ring(wk)
    hy, hx = YB // 2, XB // 2
    factor = D ** (-0.5)

    def dev(yy, xx, zz, cc):
        return (wk, ((yy * 4 + xx) * 2 + zz) * 2 + cc)

    sib = dev(y, x, z, 1 - c)
    zsame = dev(y, x, 1 - z, c)
    zother = dev(y, x, 1 - z, 1 - c)
    xright, xleft = dev(y, xr, z, c), dev(y, xl, z, c)
    yright, yleft = dev(yr, x, z, c), dev(yl, x, z, c)
    xopp, yopp = dev(y, xo, z, c), dev(yo, x, z, c)
    wright, wleft = (wr_i, me), (wl_i, me)

    pending = []

    def send(src, dst, to):
        k = len(pending)
        copy = pltpu.make_async_remote_copy(
            src_ref=src, dst_ref=dst, send_sem=ssem.at[k], recv_sem=rsem.at[k],
            device_id=to, device_id_type=MESH,
        )
        copy.start()
        pending.append(copy)
        return copy

    started = []

    def local(src, dst):
        copy = pltpu.make_async_copy(src, dst, lsem.at[len(started)])
        copy.start()
        started.append(copy)
        return copy

    def arrived(*copies):
        for copy in copies:
            copy.wait_recv()

    def cols(j):
        return pl.ds(pl.multiple_of(j * HALF, HALF), HALF)

    def wcols(j):
        return pl.ds(pl.multiple_of(j * WC, 128), WC)

    def half(ref, h):
        return ref.at[:, h * WH:(h + 1) * WH]

    def xrows(j):
        return pl.ds(pl.multiple_of(j * XB, 16), XB)

    def xrows_half(j, h):
        return pl.ds(pl.multiple_of(j * XB + h * hx, 16), hx)

    own_w = local(w_in.at[:, cols(c)], wraw.at[z, c])
    frag = {}
    for name, j in (("o", wo_i), ("r", wr_i), ("l", wl_i), ("s", wk)):
        frag[name] = (
            local(loc_in.at[:, wcols(j)], loc.at[j]),
            local(anc_in.at[:, wcols(j)], anc.at[j]),
        )
    own_x = local(x_in, xs.at[0])
    own_g = local(g_in.at[:, cols(c)], gs.at[0])
    own_m = local(mom_in, mom)

    barrier = pltpu.get_barrier_semaphore()
    partners = (sib, zsame, zother, xright, xleft, xopp, yright, yleft, yopp, wright, wleft)
    for p in partners:
        pl.semaphore_signal(barrier, inc=1, device_id=p, device_id_type=MESH)
    pl.semaphore_wait(barrier, len(partners))

    g1 = send(w_in.at[:, cols(c)], wraw.at[z, c], zsame)
    g2 = send(w_in.at[:, cols(1 - c)], wraw.at[z, c], zother)
    g0 = send(w_in.at[:, cols(1 - c)], wraw.at[z, c], sib)

    def code_block(name, j):
        for copy in frag[name]:
            copy.wait()

        def body(i, carry):
            def at(g):
                return pl.ds(pl.multiple_of((i * (4 * SETS) + g) * 128, 128), 128)

            def delta_at(g):
                return anc[j, :, at(g)].astype(F32) - loc[j, :, at(g)].astype(F32)

            def store(g, value):
                cod[j, :, at(g)] = value

            code_chunk(delta_at, store)
            return carry

        lax.fori_loop(0, WC // (512 * SETS), body, 0)

    state = [{}, {}]

    def gather1(s):
        mine_a, mine_b = wa.at[s, y, xrows(x)], wb.at[s, y, xrows(x)]
        out = []
        for a_to, b_to in ((xright, yright), (xleft, yleft), (xopp, yopp)):
            out.append(send(mine_a, mine_a, a_to))
            out.append(send(mine_b, mine_b, b_to))
        state[s]["g1"] = out

    def gather2(s):
        st = state[s]
        arrived(*st["g1"])
        a = (wa.at[s, y, 0:hy], wa.at[s, y, hy:YB])
        b = (wb.at[s, 0:2, xrows(x)], wb.at[s, 2:4, xrows(x)])
        st["g2"] = (
            send(a[0], a[0], yright), send(b[0], b[0], xright),
            send(a[1], a[1], yleft), send(b[1], b[1], xleft),
        )
        st["g3"] = [
            send(a[1], a[1], yright), send(b[1], b[1], xright),
            send(a[0], a[0], yleft), send(b[0], b[0], xleft),
        ]

    def gather2_next(s):
        st = state[s]
        steps = (
            (wa.at[s, yl, 0:hy], yright), (wb.at[s, 0:2, xrows(xl)], xright),
            (wa.at[s, yr, hy:YB], yleft), (wb.at[s, 2:4, xrows(xr)], xleft),
        )
        for copy, (ref, to) in zip(st["g2"], steps):
            arrived(copy)
            st["g3"].append(send(ref, ref, to))

    def forward(s, t):
        if t == 0:
            arrived(*state[s]["g3"])

        def body(i, carry):
            r = pl.ds(pl.multiple_of(i * 256, 256), 256)
            weight = jnp.concatenate([wa[s].reshape(D, R), wb[s].reshape(D, R)], axis=1)
            value = jnp.dot(xs[t, r, :], weight, preferred_element_type=F32) * factor
            sig = jax.nn.sigmoid(value)
            cot = gs[t, r, 2 * R * s:2 * R * (s + 1)].astype(F32)
            act[s, t, r, :] = (cot * sig * (1.0 + value * (1.0 - sig))).astype(BF16)
            return carry

        lax.fori_loop(0, 2, body, 0)

    def backward(s, yy, slot):
        at = pl.ds(pl.multiple_of(yy * YB, 128), YB)
        dims = (((0,), (0,)), ((), ()))
        part = lax.dot_general(xs[0, :, at], act[s, 0], dims, preferred_element_type=F32)
        part += lax.dot_general(xs[1, :, at], act[s, 1], dims, preferred_element_type=F32)
        pa[s, yy] = part[:, :R].astype(BF16)
        pb[s, slot] = part[:, R:].astype(BF16)

    def reduce1(s):
        st = state[s]
        backward(s, yo, 0)
        a0 = send(pa.at[s, yo, 0:hy], ra_o.at[s, 0], yright)
        a1 = send(pa.at[s, yo, hy:YB], ra_o.at[s, 1], yleft)
        backward(s, yr, 1)
        b0 = send(pb.at[s, 0:2, xrows(xo)], rb_o.at[s, 0], xright)
        b3 = send(pb.at[s, 0:2, xrows(xl)], rb_r.at[s, 0:2], xleft)
        a2 = send(pa.at[s, yr, hy:YB], ra_l.at[s, hy:YB], yright)
        backward(s, yl, 2)
        a3 = send(pa.at[s, yl, 0:hy], ra_r.at[s, 0:hy], yleft)
        backward(s, y, 3)
        b1 = send(pb.at[s, 2:4, xrows(xo)], rb_o.at[s, 1], xleft)
        b2 = send(pb.at[s, 2:4, xrows(xr)], rb_l.at[s, 2:4], xright)
        st["r1"] = (a0, a1, b0, b1)
        st["ra"], st["rb"] = [a2, a3], [b2, b3]

    def add_to(dst, at, other, n):
        def body(i, carry):
            r = pl.ds(pl.multiple_of(i * 96, 16), 96)
            d = pl.ds(pl.multiple_of(at + i * 96, 16), 96)
            dst[d, :] = (dst[d, :].astype(F32) + other[r, :].astype(F32)).astype(BF16)
            return carry

        lax.fori_loop(0, n // 96, body, 0)

    def reduce1_next(s):
        st = state[s]
        a0, a1, b0, b1 = st["r1"]
        arrived(a0)
        add_to(pa.at[s, yr], 0, ra_o.at[s, 0], hy)
        st["ra"].append(send(pa.at[s, yr, 0:hy], ra_l.at[s, 0:hy], yright))
        arrived(a1)
        add_to(pa.at[s, yl], hy, ra_o.at[s, 1], hy)
        st["ra"].append(send(pa.at[s, yl, hy:YB], ra_r.at[s, hy:YB], yleft))
        arrived(b0)
        for k in range(2):
            add_to(pb.at[s, k], xr * XB, rb_o.at[s, 0, k], XB)
        st["rb"].append(send(pb.at[s, 0:2, xrows(xr)], rb_l.at[s, 0:2], xright))
        arrived(b1)
        for k in range(2):
            add_to(pb.at[s, 2 + k], xl * XB, rb_o.at[s, 1, k], XB)
        st["rb"].append(send(pb.at[s, 2:4, xrows(xl)], rb_r.at[s, 2:4], xleft))

    def reduce2(s):
        st = state[s]
        arrived(*st["ra"])

        def sum_a(i, carry):
            r = pl.ds(pl.multiple_of(i * 192, 96), 192)
            total = pa[s, y, r, :].astype(F32) + ra_l[s, r, :].astype(F32) + ra_r[s, r, :].astype(F32)
            sa[s, r, :] = total
            sa16[s, r, :] = total.astype(BF16)
            return carry

        lax.fori_loop(0, YB // 192, sum_a, 0)
        st["ta"] = [
            send(sa16.at[s, xrows(j)], ta.at[s, k], to)
            for k, (j, to) in enumerate(((xo, xopp), (xr, xright), (xl, xleft)))
        ]
        arrived(*st["rb"])

        def sum_b(k, carry):
            total = pb[s, k, xrows(x), :].astype(F32) + rb_l[s, k].astype(F32) + rb_r[s, k].astype(F32)
            sb[s, k] = total
            sb16[s, k] = total.astype(BF16)
            return carry

        lax.fori_loop(0, 4, sum_b, 0)
        st["tb"] = [
            send(sb16.at[s, k], tb.at[s, k], to) for k, to in enumerate((yopp, yright, yleft))
        ]

    def part(zz, cc):
        return pl.ds(pl.multiple_of((zz * 2 + cc) * ROWS, 8), ROWS)

    def reduce3(s):
        st = state[s]
        arrived(*st["ta"])
        tt[s, :, 0:R] = sa[s, xrows(x), :] + (
            ta[s, 0].astype(F32) + ta[s, 1].astype(F32) + ta[s, 2].astype(F32)
        )
        arrived(*st["tb"])
        tt[s, :, R:2 * R] = sb[s, 3] + (
            tb[s, 0].astype(F32) + tb[s, 1].astype(F32) + tb[s, 2].astype(F32)
        )
        for k in range(2):
            fz_send[s, k] = tt[s, part(1 - z, k), :].astype(BF16)
        f1 = send(fz_send.at[s, c], fz_recv.at[s, c], zsame)
        f2 = send(fz_send.at[s, 1 - c], fz_recv.at[s, c], zother)
        fs_send[s] = tt[s, part(z, 1 - c), :]
        f0 = send(fs_send.at[s], fs_recv.at[s], sib)
        st["f"] = (f1, f2, f0)

    def last(s):
        arrived(*state[s]["f"])

        def at(j):
            return pl.ds(pl.multiple_of(j * HALF + 2 * R * s, 2 * R), 2 * R)

        wg_v[:, at(c)] = (tt[s, part(z, c), :] + fz_recv[s, c].astype(F32)) * factor
        wg_v[:, at(1 - c)] = (fs_recv[s] + fz_recv[s, 1 - c].astype(F32)) * factor

    code_block("o", wo_i)

    own_w.wait()
    arrived(g1, g2, g0)
    for zz in range(2):
        rows = jnp.concatenate(
            [wraw[zz, 0].astype(F32), wraw[zz, 1].astype(F32)], axis=0
        ).astype(BF16)
        for s in range(2):
            wa[s, y, xrows_half(x, zz), :] = rows[:, 2 * R * s:2 * R * s + R]
            wb[s, y, xrows_half(x, zz), :] = rows[:, 2 * R * s + R:2 * R * (s + 1)]

    gather1(0)
    gather1(1)
    w0 = send(half(cod.at[wo_i], 0), wo.at[0], wright)
    w1 = send(half(cod.at[wo_i], 1), wo.at[1], wleft)
    sx = send(x_in, xs.at[1], sib)
    sg = send(g_in.at[:, cols(1 - c)], gs.at[1], sib)

    code_block("r", wr_i)
    w2 = send(half(cod.at[wr_i], 1), half(wl, 1), wright)
    gather2(0)
    code_block("l", wl_i)
    w3 = send(half(cod.at[wl_i], 0), half(wr, 0), wleft)
    gather2_next(0)
    gather2(1)
    code_block("s", wk)

    own_x.wait()
    own_g.wait()
    arrived(sx, sg)
    forward(0, 0)
    gather2_next(1)
    forward(0, 1)
    reduce1(0)

    arrived(w0, w1)
    for j, h in ((wr_i, 0), (wl_i, 1)):
        def body(i, carry, j=j, h=h):
            at = pl.ds(pl.multiple_of(i * 256, 256), 256)
            to = pl.ds(pl.multiple_of(h * WH + i * 256, 256), 256)
            cod[j, :, to] = (cod[j, :, to].astype(F32) + wo[h, :, at].astype(F32)).astype(BF16)
            return carry
        lax.fori_loop(0, WH // 256, body, 0)
    w4 = send(half(cod.at[wr_i], 0), half(wl, 0), wright)
    w5 = send(half(cod.at[wl_i], 1), half(wr, 1), wleft)

    forward(1, 0)
    forward(1, 1)
    reduce1_next(0)
    reduce1(1)
    reduce2(0)
    reduce1_next(1)

    arrived(w2, w3, w4, w5)
    own_m.wait()

    def outer(i, carry):
        at = pl.ds(pl.multiple_of(i * 256, 256), 256)
        total = cod[wk, :, at].astype(F32) + wl[:, at].astype(F32) + wr[:, at].astype(F32)
        grad = total * 0.25
        fresh = 0.9 * mom[:, at] + grad
        nm_v[:, at] = fresh
        na_v[:, at] = (anc[wk, :, at].astype(F32) - 0.7 * (grad + 0.9 * fresh)).astype(BF16)
        return carry

    lax.fori_loop(0, WC // 256, outer, 0)
    out1 = local(na_v, na_out)
    out2 = local(nm_v, nm_out)

    reduce2(1)
    reduce3(0)
    reduce3(1)
    last(0)
    last(1)
    out0 = local(wg_v, wg_out)
    for copy in pending:
        copy.wait_send()
    for copy in (out0, out1, out2):
        copy.wait()


def hand_on(wg_in, na_in, nm_in, wg_out, na_out, nm_out, wg_v, na_v, nm_v, sem):
    h = WC // 4
    parts = [
        (a.at[:, k * h:(k + 1) * h], v.at[:, k * h:(k + 1) * h], b.at[:, k * h:(k + 1) * h])
        for a, v, b in ((nm_in, nm_v, nm_out), (na_in, na_v, na_out))
        for k in range(4)
    ] + [(wg_in, wg_v, wg_out)]
    reads = [pltpu.make_async_copy(a, v, sem.at[0, k]) for k, (a, v, b) in enumerate(parts)]
    writes = [pltpu.make_async_copy(v, b, sem.at[1, k]) for k, (a, v, b) in enumerate(parts)]
    for copy in reads:
        copy.start()
    for read, write in zip(reads, writes):
        read.wait()
        write.start()
    for copy in writes:
        copy.wait()


def shards(inner_input, inner_weight, grad_out, local_fragment, anchor, momentum):
    any_spec = pl.BlockSpec(memory_space=pl.ANY)
    vm = pltpu.VMEM
    hy, hx = YB // 2, XB // 2
    wg, na, nm = pl.pallas_call(
        kernel,
        out_shape=(
            jax.ShapeDtypeStruct((ROWS, 1024), F32),
            jax.ShapeDtypeStruct((ROWS, WC), BF16),
            jax.ShapeDtypeStruct((ROWS, WC), F32),
        ),
        in_specs=[any_spec] * 6,
        out_specs=(any_spec,) * 3,
        scratch_shapes=[
            vm((2, TOK, D), BF16), vm((2, TOK, HALF), BF16), vm((2, 2, ROWS, HALF), BF16),
            vm((2, 4, YB, R), BF16), vm((2, 4, YB, R), BF16),
            vm((2, 2, TOK, 2 * R), BF16),
            vm((2, 4, YB, R), BF16), vm((2, 4, YB, R), BF16),
            vm((2, 2, hy, R), BF16), vm((2, YB, R), BF16), vm((2, YB, R), BF16),
            vm((2, 2, 2, XB, R), BF16), vm((2, 4, XB, R), BF16), vm((2, 4, XB, R), BF16),
            vm((2, YB, R), F32), vm((2, 4, XB, R), F32), vm((2, YB, R), BF16), vm((2, 4, XB, R), BF16),
            vm((2, 3, XB, R), BF16), vm((2, 3, XB, R), BF16),
            vm((2, XB, 2 * R), F32),
            vm((2, ROWS, 2 * R), F32), vm((2, ROWS, 2 * R), F32),
            vm((2, 2, ROWS, 2 * R), BF16), vm((2, 2, ROWS, 2 * R), BF16),
            vm((ROWS, 1024), F32),
            vm((4, ROWS, WC), BF16), vm((4, ROWS, WC), BF16), vm((ROWS, WC), F32),
            vm((4, ROWS, WC), BF16),
            vm((2, ROWS, WH), BF16), vm((ROWS, WC), BF16), vm((ROWS, WC), BF16),
            vm((ROWS, WC), BF16), vm((ROWS, WC), F32),
            pltpu.SemaphoreType.DMA((16,)),
            pltpu.SemaphoreType.DMA((100,)),
            pltpu.SemaphoreType.DMA((100,)),
        ],
        compiler_params=pltpu.CompilerParams(
            collective_id=0, has_side_effects=True, vmem_limit_bytes=60 * 1024 * 1024
        ),
        cost_estimate=pl.CostEstimate(
            flops=4 * TOK * D * 1024, bytes_accessed=16 * 1024 * 1024, transcendentals=TOK * 1024
        ),
    )(inner_input[0], inner_weight[0], grad_out[0], local_fragment[0], anchor, momentum)
    wg, na, nm = pl.pallas_call(
        hand_on,
        out_shape=tuple(jax.ShapeDtypeStruct(a.shape, a.dtype) for a in (wg, na, nm)),
        in_specs=[any_spec] * 3,
        out_specs=(any_spec,) * 3,
        scratch_shapes=[vm(a.shape, a.dtype) for a in (wg, na, nm)] + [pltpu.SemaphoreType.DMA((2, 9))],
    )(wg, na, nm)
    return (wg[None], na, nm)


def solution(mesh):
    in_specs = (
        P("worker", "fsdp", None),
        P("worker", "fsdp", None),
        P("worker", "fsdp", None),
        P("worker", "fsdp", None),
        P("fsdp", None),
        P("fsdp", "worker"),
    )
    out_specs = (P("worker", "fsdp", None), P("fsdp", "worker"), P("fsdp", "worker"))
    return jax.shard_map(shards, mesh=mesh, in_specs=in_specs, out_specs=out_specs, check_vma=False)
```
